32 devices in a mesh: img: 4 (over y, x), sp: 8 (over z, core).
Axes of the slice: x: 2, y: 2, z: 4, core: 2. Of those that a mesh axis runs over, the one named last changes fastest.
Arguments:
- tokens: bfloat16 [4, 7168, 2240], P('img', 'sp'), may hold values from -12 to 12
- queries: bfloat16 [4, 7168, 1120], P('img', 'sp'), may hold values from -6 to 6
- w_key: bfloat16 [2240, 1120], P('img'), may hold values from -0.125 to 0.125
- w_value: bfloat16 [2240, 1120], P('img'), may hold values from -0.125 to 0.125
- cotangent: bfloat16 [4, 7168, 1120], P('img', 'sp'), may hold values from -6 to 6
Outputs:
- attended: bfloat16 [4, 7168, 1120], P('img', 'sp')
- d_tokens: bfloat16 [4, 7168, 2240], P('img', 'sp')
- d_queries: bfloat16 [4, 7168, 1120], P('img', 'sp')
- d_w_key: float32 [2240, 1120], P('img')
- d_w_value: float32 [2240, 1120], P('img')
The draws below stay inside these ranges and needn't reach their ends.
All inputs are finite; a program needn't handle non-finite values.
Results may differ from the reference program's by a relative error of at most 0.006.
Values may be sent and summed in bfloat16 or wider, within the bound.
No kernel may reach another device: no remote copies, remote signals or barrier semaphores. Data moves between devices by JAX's collectives and lax.ppermute only.
A program may use at most 128 MiB of HBM per device.

```python
import jax
import jax.numpy as jnp
from jax import lax

D = 2240
HEADS = 35
HD = 32
TOK_DEV = 896
HK = 1120
TOK_IMG = 7168
IMAGES = 4


def draw_tokens(key, part):
    first = jax.random.fold_in(key, 11)
    tiles = TOK_IMG // TOK_DEV
    rough = jnp.clip(jax.random.normal(first, (IMAGES, tiles, TOK_DEV, D), jnp.float32), -4.0, 4.0)
    rise = 1.0 + 2.0 * jnp.arange(tiles, dtype=jnp.float32) / max(tiles - 1, 1)
    values = rise.reshape(1, tiles, 1, 1) * rough
    return values.reshape(IMAGES, TOK_IMG, D).astype(jnp.bfloat16)


def level_of(rng, dims, split, least, largest):
    gain = 1.0
    for axis_at, blocks in split:
        draws = jax.random.uniform(jax.random.fold_in(jax.random.fold_in(rng, 6), axis_at), (blocks,), jnp.float32, least / len(split), largest / len(split))
        gain = gain * jnp.repeat(jnp.exp(draws), dims[axis_at] // blocks).reshape((-1,) + (1,) * (len(dims) - 1 - axis_at))
    return gain


def noise(key, shape, scale, most, shards=(), kind=jnp.bfloat16):
    entries = scale * jax.random.normal(key, shape, jnp.float32)
    if shards:
        entries = entries * level_of(key, shape, shards, -0.22, 0.18)
    return jnp.clip(entries, -most, most).astype(kind)


def setup_inputs(seed: int = 0) -> dict:
    arg_keys = jax.random.split(jax.random.key(seed), 6)
    return {
        "tokens": draw_tokens(jax.random.fold_in(arg_keys[5], 71), 0),
        "queries": noise(arg_keys[1], (IMAGES, TOK_IMG, HK), 1.0, 6.0, ((0, 4), (1, 8))),
        "w_key": noise(arg_keys[2], (D, HK), D ** -0.5, 0.125, ((0, 4),)),
        "w_value": noise(arg_keys[3], (D, HK), D ** -0.5, 0.125, ((0, 4),)),
        "cotangent": noise(arg_keys[4], (IMAGES, TOK_IMG, HK), 1.0, 6.0, ((0, 4), (1, 8))),
    }


EPS_DEN = 1e-06

def reference(tokens, queries, w_key, w_value, cotangent):
    high = lax.Precision.HIGHEST
    flat = tokens.reshape(-1, D)
    key_pre = jnp.dot(flat, w_key, preferred_element_type=jnp.float32)
    key_feat = jnp.maximum(key_pre, 0.0).astype(jnp.bfloat16)
    val_feat = jnp.dot(flat, w_value, preferred_element_type=jnp.float32).astype(jnp.bfloat16)
    key_f32 = key_feat.astype(jnp.float32).reshape(IMAGES, TOK_IMG, HEADS, HD)
    val_f32 = val_feat.astype(jnp.float32).reshape(IMAGES, TOK_IMG, HEADS, HD)
    kv_state = jnp.einsum('nthi,nthj->nhij', key_f32, val_f32, precision=high)
    key_norm = lax.optimization_barrier(jnp.sum(key_f32, axis=1))
    q_feat = jnp.maximum(queries.astype(jnp.float32), 0.0).reshape(IMAGES, TOK_IMG, HEADS, HD)
    numerator = jnp.einsum('nthi,nhij->nthj', q_feat, kv_state, precision=high)
    denominator = jnp.einsum('nthi,nhi->nth', q_feat, key_norm, precision=high) + EPS_DEN
    attn_f32 = numerator / denominator[..., None]
    attended = attn_f32.astype(jnp.bfloat16).reshape(IMAGES, TOK_IMG, HK)
    cot_f32 = cotangent.astype(jnp.float32).reshape(IMAGES, TOK_IMG, HEADS, HD)
    d_num = cot_f32 / denominator[..., None]
    d_den = -lax.optimization_barrier(jnp.sum(cot_f32 * attn_f32, axis=-1)) / denominator
    d_feat = jnp.einsum('nthj,nhij->nthi', d_num, kv_state, precision=high) + d_den[..., None] * key_norm[:, None]
    d_queries = jnp.where(q_feat > 0, d_feat, 0.0).astype(jnp.bfloat16).reshape(IMAGES, TOK_IMG, HK)
    grad_state = TOK_IMG * jnp.einsum('nthi,nthj->nhij', q_feat, d_num, precision=high)
    grad_norm = TOK_IMG * jnp.einsum('nth,nthi->nhi', d_den, q_feat, precision=high)
    d_key_f = jnp.einsum('nthj,nhij->nthi', val_f32, grad_state, precision=high) + grad_norm[:, None]
    d_key = jnp.where(key_f32 > 0, d_key_f, 0.0).astype(jnp.bfloat16).reshape(-1, HK)
    d_value = jnp.einsum('nthi,nhij->nthj', key_f32, grad_state, precision=high).astype(jnp.bfloat16).reshape(-1, HK)
    d_flat = jnp.dot(d_key, w_key.T, preferred_element_type=jnp.float32) + jnp.dot(d_value, w_value.T, preferred_element_type=jnp.float32)
    d_tokens = d_flat.astype(jnp.bfloat16).reshape(IMAGES, TOK_IMG, D)
    scale = 1.0 / jnp.sqrt(jnp.float32(IMAGES * TOK_IMG))
    d_w_key = jnp.dot(flat.T, d_key, preferred_element_type=jnp.float32) * scale
    d_w_value = jnp.dot(flat.T, d_value, preferred_element_type=jnp.float32) * scale
    return (attended, d_tokens, d_queries, d_w_key, d_w_value)
```

```python
import functools

import jax
import jax.numpy as jnp
from jax import lax
from jax.experimental import pallas as pl
from jax.experimental.pallas import tpu as pltpu
from jax.sharding import PartitionSpec as P

HD = 32
EPS_DEN = 1e-06
LANES = 256
STATE_ROWS = 40
BF, F32 = jnp.bfloat16, jnp.float32
VMEM_LIMIT = 48 * 1024 * 1024


def dot(a, b, ca, cb):
    return lax.dot_general(a, b, (((ca,), (cb,)), ((), ())), preferred_element_type=F32)


def tiles_of(width):
    return [(s, min(LANES, width - s)) for s in range(0, width, LANES)]


def same_head(w):
    row = lax.broadcasted_iota(jnp.int32, (w, w), 0) // HD
    col = lax.broadcasted_iota(jnp.int32, (w, w), 1) // HD
    return row == col


def fold(full, w):
    kept = jnp.where(same_head(w), full, 0.0)
    total = kept[0:HD]
    for at in range(HD, w, HD):
        total = total + kept[at : at + HD]
    return total


def unfold(rows, w):
    return jnp.where(same_head(w), jnp.concatenate([rows] * (w // HD), axis=0), 0.0)


def split(x):
    high = x.astype(BF)
    return high, (x - high.astype(F32)).astype(BF)


def params(**kw):
    return pltpu.CompilerParams(vmem_limit_bytes=VMEM_LIMIT, **kw)


def place_copies(scal, refs, places, bufs, sems):
    copies = []
    for n, (ref, (which, rel, off, shard)) in enumerate(zip(refs, places)):
        if rel is None:
            start = off
        else:
            start = pl.multiple_of((scal[0] ^ rel) * shard + off, 16)
        copies.append(
            pltpu.make_async_copy(ref, bufs[which].at[pl.ds(start, ref.shape[0]), :], sems.at[n])
        )
    return copies


def proj_kernel(places, width, scal, tok, *refs):
    pieces = refs[: len(places)]
    k_out, v_out, st_out, w_a, w_b, sems = refs[len(places) :]
    step = pl.program_id(0)

    @pl.when(step == 0)
    def _():
        copies = place_copies(scal, pieces, places, (w_a, w_b), sems)
        for c in copies:
            c.start()
        for c in copies:
            c.wait()
        st_out[...] = jnp.zeros_like(st_out)

    first = scal[1] == 0
    rows = tok[...]
    a = dot(rows, w_a[...], 1, 0)
    b = dot(rows, w_b[...], 1, 0)
    key = jnp.maximum(jnp.where(first, a, b), 0.0)
    val = jnp.where(first, b, a)
    k_out[...] = key.astype(BF)
    v_out[...] = val.astype(BF)
    for s, w in tiles_of(width):
        cols = slice(s, s + w)
        k, v = k_out[:, cols], v_out[:, cols]
        st_out[0:HD, cols] += fold(dot(v, k, 0, 0), w)
        st_out[HD : HD + 1, cols] += jnp.sum(k.astype(F32), axis=0, keepdims=True)


def project(scal, tok, pieces, places, width, tile):
    count, depth = tok.shape
    grid = count // tile
    return pl.pallas_call(
        functools.partial(proj_kernel, places, width),
        grid_spec=pltpu.PrefetchScalarGridSpec(
            num_scalar_prefetch=1,
            grid=(grid,),
            in_specs=[pl.BlockSpec((tile, depth), lambda i, s: (i, 0))]
            + [pl.BlockSpec(memory_space=pl.ANY)] * len(pieces),
            out_specs=[
                pl.BlockSpec((tile, width), lambda i, s: (i, 0)),
                pl.BlockSpec((tile, width), lambda i, s: (i, 0)),
                pl.BlockSpec((STATE_ROWS, width), lambda i, s: (0, 0)),
            ],
            scratch_shapes=[
                pltpu.VMEM((depth, width), BF),
                pltpu.VMEM((depth, width), BF),
                pltpu.SemaphoreType.DMA((len(pieces),)),
            ],
        ),
        out_shape=[
            jax.ShapeDtypeStruct((count, width), BF),
            jax.ShapeDtypeStruct((count, width), BF),
            jax.ShapeDtypeStruct((STATE_ROWS, width), F32),
        ],
        compiler_params=params(dimension_semantics=("arbitrary",)),
        cost_estimate=pl.CostEstimate(
            flops=4 * count * depth * width, bytes_accessed=2 * count * depth + 4 * depth * width, transcendentals=0
        ),
        name="project",
    )(scal, tok, *pieces)


def attend_kernel(off, width, n_prev, q_ref, g_ref, st, *refs):
    prev = refs[: 2 * n_prev]
    att_out, dq_out, gs_out, kv_hi, kv_lo, kn_hi, kn_lo = refs[2 * n_prev :]
    step = pl.program_id(0)
    tiles = tiles_of(width)

    @pl.when(step == 0)
    def _():
        gs_out[...] = jnp.zeros_like(gs_out)
        for n, (s, w) in enumerate(tiles):
            kv = unfold(st[0:HD, s : s + w], w)
            kn = unfold(jnp.broadcast_to(st[HD : HD + 1, s : s + w], (HD, w)), w)
            kv_hi[n, 0:w, 0:w], kv_lo[n, 0:w, 0:w] = split(kv)
            kn_hi[n, 0:w, 0:w], kn_lo[n, 0:w, 0:w] = split(kn)

    at = 0
    for n in range(n_prev):
        w = prev[2 * n].shape[1]
        att_out[:, at : at + w] = prev[2 * n][...]
        dq_out[:, at : at + w] = prev[2 * n + 1][...]
        at += w
    for n, (s, w) in enumerate(tiles):
        q = jnp.maximum(q_ref[:, off + s : off + s + w], 0)
        g = g_ref[:, off + s : off + s + w].astype(F32)
        h, l = kv_hi[n, 0:w, 0:w], kv_lo[n, 0:w, 0:w]
        num = dot(q, h, 1, 1) + dot(q, l, 1, 1)
        den = dot(q, kn_hi[n, 0:w, 0:w], 1, 1) + dot(q, kn_lo[n, 0:w, 0:w], 1, 1) + EPS_DEN
        inv = 1.0 / den
        attn = num * inv
        dn = g * inv
        ones = jnp.where(same_head(w), 1.0, 0.0).astype(BF)
        ga_hi, ga_lo = split(g * attn)
        dden = -(dot(ga_hi, ones, 1, 0) + dot(ga_lo, ones, 1, 0)) * inv
        dn_hi, dn_lo = split(dn)
        df = dot(dn_hi, h, 1, 0) + dot(dn_hi, l, 1, 0) + dot(dn_lo, h, 1, 0)
        df = df + dden * st[HD : HD + 1, s : s + w]
        q32 = q.astype(F32)
        att_out[:, at + s : at + s + w] = attn.astype(BF)
        dq_out[:, at + s : at + s + w] = jnp.where(q32 > 0, df, 0.0).astype(BF)
        gs_out[0:HD, s : s + w] += fold(dot(dn_hi, q, 0, 0) + dot(dn_lo, q, 0, 0), w)
        gs_out[HD : HD + 1, s : s + w] += jnp.sum(dden * q32, axis=0, keepdims=True)


def attend(queries, cotangent, state, off, width, prev, tile):
    count, full = queries.shape
    n_prev = len(prev) // 2
    tiles = len(tiles_of(width))
    wide = width + sum(p.shape[1] for p in prev[::2])
    row = lambda w: pl.BlockSpec((tile, w), lambda i: (i, 0))
    return pl.pallas_call(
        functools.partial(attend_kernel, off, width, n_prev),
        grid=(count // tile,),
        in_specs=[row(full), row(full), pl.BlockSpec((STATE_ROWS, width), lambda i: (0, 0))]
        + [row(p.shape[1]) for p in prev],
        out_specs=[row(wide), row(wide), pl.BlockSpec((STATE_ROWS, width), lambda i: (0, 0))],
        out_shape=[
            jax.ShapeDtypeStruct((count, wide), BF),
            jax.ShapeDtypeStruct((count, wide), BF),
            jax.ShapeDtypeStruct((STATE_ROWS, width), F32),
        ],
        scratch_shapes=[pltpu.VMEM((tiles, LANES, LANES), BF)] * 4,
        compiler_params=params(dimension_semantics=("arbitrary",)),
        cost_estimate=pl.CostEstimate(
            flops=24 * count * width * LANES, bytes_accessed=8 * count * full, transcendentals=0
        ),
        name="attend",
    )(queries, cotangent, state, *prev)


def feat_kernel(width, scale, scal, k_ref, v_ref, st, keep, send, gs_hi, gs_lo):
    tiles = tiles_of(width)

    @pl.when(pl.program_id(0) == 0)
    def _():
        for n, (s, w) in enumerate(tiles):
            gs = unfold(st[0:HD, s : s + w] * scale, w)
            gs_hi[n, 0:w, 0:w], gs_lo[n, 0:w, 0:w] = split(gs)

    first = scal[1] == 0
    for n, (s, w) in enumerate(tiles):
        cols = slice(s, s + w)
        k, v = k_ref[:, cols], v_ref[:, cols]
        h, l = gs_hi[n, 0:w, 0:w], gs_lo[n, 0:w, 0:w]
        dv = dot(k, h, 1, 1) + dot(k, l, 1, 1)
        dk = dot(v, h, 1, 0) + dot(v, l, 1, 0) + st[HD : HD + 1, cols] * scale
        dk = jnp.where(k.astype(F32) > 0, dk, 0.0)
        keep[:, cols] = jnp.where(first, dk, dv).astype(BF)
        send[:, cols] = jnp.where(first, dv, dk).astype(BF)


def feature_grads(scal, key, val, state, scale, tile):
    count, width = key.shape
    tiles = len(tiles_of(width))
    row = pl.BlockSpec((tile, width), lambda i, s: (i, 0))
    return pl.pallas_call(
        functools.partial(feat_kernel, width, scale),
        grid_spec=pltpu.PrefetchScalarGridSpec(
            num_scalar_prefetch=1,
            grid=(count // tile,),
            in_specs=[row, row, pl.BlockSpec((STATE_ROWS, width), lambda i, s: (0, 0))],
            out_specs=[row, row],
            scratch_shapes=[pltpu.VMEM((tiles, LANES, LANES), BF)] * 2,
        ),
        out_shape=[jax.ShapeDtypeStruct((count, width), BF)] * 2,
        compiler_params=params(dimension_semantics=("arbitrary",)),
        cost_estimate=pl.CostEstimate(
            flops=8 * count * width * LANES, bytes_accessed=8 * count * width, transcendentals=0
        ),
        name="feature_grads",
    )(scal, key, val, state)


def weight_kernel(cut, scal, t_own, t_other, d_own, d_other, send_a, send_b, keep_a, keep_b):
    step = pl.program_id(0)
    part = dot(t_own[...], d_own[...], 1, 0) + dot(t_other[...], d_other[...], 1, 0)
    a, b = part[:cut], part[cut:]

    @pl.when(step == 0)
    def _():
        send_a[1] = a.astype(BF)
        send_b[1] = b.astype(BF)

    @pl.when(step == 1)
    def _():
        send_b[0] = b.astype(BF)
        keep_a[1] = a

    @pl.when(step == 2)
    def _():
        send_a[0] = a.astype(BF)
        keep_b[1] = b

    @pl.when(step == 3)
    def _():
        keep_a[0] = a
        keep_b[0] = b


def weight_grads(scal, t_own, t_other, d_own, d_other, shard, cut):
    depth, count = t_own.shape
    width = d_own.shape[1]
    at = lambda i, s: ((3 - i) ^ s[0], 0)
    rows = pl.BlockSpec((shard, count), at)
    whole = pl.BlockSpec((count, width), lambda i, s: (0, 0))
    full = lambda r: pl.BlockSpec((2, r, width), lambda i, s: (0, 0, 0))
    rest = shard - cut
    return pl.pallas_call(
        functools.partial(weight_kernel, cut),
        grid_spec=pltpu.PrefetchScalarGridSpec(
            num_scalar_prefetch=1,
            grid=(4,),
            in_specs=[rows, rows, whole, whole],
            out_specs=[full(cut), full(rest), full(cut), full(rest)],
        ),
        out_shape=[
            jax.ShapeDtypeStruct((2, cut, width), BF),
            jax.ShapeDtypeStruct((2, rest, width), BF),
            jax.ShapeDtypeStruct((2, cut, width), F32),
            jax.ShapeDtypeStruct((2, rest, width), F32),
        ],
        compiler_params=params(dimension_semantics=("arbitrary",)),
        cost_estimate=pl.CostEstimate(
            flops=4 * count * depth * width, bytes_accessed=4 * count * depth + 6 * depth * width, transcendentals=0
        ),
        name="weight_grads",
    )(scal, t_own, t_other, d_own, d_other)


def input_kernel(plan, scal, *refs):
    n_d = 2 * len(plan)
    n_w = sum(len(places) for places, _ in plan)
    grads, pieces = refs[:n_d], refs[n_d : n_d + n_w]
    out = refs[n_d + n_w]
    bufs = refs[n_d + n_w + 1 : n_d + n_w + 1 + n_d]
    sems = refs[-1]

    @pl.when(pl.program_id(0) == 0)
    def _():
        copies, at = [], 0
        for n, (places, _) in enumerate(plan):
            here = pieces[at : at + len(places)]
            copies += place_copies(scal, here, places, bufs[2 * n : 2 * n + 2], sems.at[pl.ds(at, len(places))])
            at += len(places)
        for c in copies:
            c.start()
        for c in copies:
            c.wait()

    total = dot(grads[0][...], bufs[0][...], 1, 1)
    for n in range(1, n_d):
        total = total + dot(grads[n][...], bufs[n][...], 1, 1)
    out[...] = total.astype(BF)


def input_grads(scal, grads, pieces, plan, depth, tile):
    count = grads[0].shape[0]
    widths = [g.shape[1] for g in grads]
    return pl.pallas_call(
        functools.partial(input_kernel, plan),
        grid_spec=pltpu.PrefetchScalarGridSpec(
            num_scalar_prefetch=1,
            grid=(count // tile,),
            in_specs=[pl.BlockSpec((tile, w), lambda i, s: (i, 0)) for w in widths]
            + [pl.BlockSpec(memory_space=pl.ANY)] * len(pieces),
            out_specs=pl.BlockSpec((tile, depth), lambda i, s: (i, 0)),
            scratch_shapes=[pltpu.VMEM((depth, w), BF) for w in widths]
            + [pltpu.SemaphoreType.DMA((len(pieces),))],
        ),
        out_shape=jax.ShapeDtypeStruct((count, depth), BF),
        compiler_params=params(dimension_semantics=("arbitrary",)),
        cost_estimate=pl.CostEstimate(
            flops=2 * count * depth * sum(widths), bytes_accessed=2 * count * depth + 2 * depth * sum(widths), transcendentals=0
        ),
        name="input_grads",
    )(scal, *grads, *pieces)


def swap(x, axis, bit):
    n = lax.axis_size(axis)
    return lax.ppermute(x, axis, [(i, i ^ bit) for i in range(n)])


def cuts_of(width):
    first = min(512, width)
    return [(0, first), (first, width - first)] if first < width else [(0, width)]


def tile_of(count):
    return next(t for t in (224, 128, 64, 32, 16) if count % t == 0)


def body_exchange(tokens, queries, w_key, w_value, cotangent):
    tok, qs, cot = tokens[0], queries[0], cotangent[0]
    count, depth = tok.shape
    shard, full = w_key.shape
    tile = tile_of(count)
    img, spx = lax.axis_index("img"), lax.axis_index("sp")
    core = spx % 2
    first = core == 0
    scal = jnp.stack([img, core]).astype(jnp.int32)
    tok_img = count * lax.axis_size("sp")
    scale = 1.0 / (lax.axis_size("img") * tok_img) ** 0.5
    cut = shard // 2 // 16 * 16

    def sum_tiles(x):
        x = x + swap(x, "sp", 1)
        x = x + swap(x, "sp", 2)
        return x + swap(x, "sp", 4)

    tok_t = tok.T
    tok_t_other = swap(tok_t, "sp", 1)

    after = None
    gathered = []
    for off, width in cuts_of(full):
        wk, wv = w_key[:, off : off + width], w_value[:, off : off + width]
        mine, theirs = jnp.where(first, wk, wv), jnp.where(first, wv, wk)
        if after is not None:
            mine, _ = lax.optimization_barrier((mine, after))
        by_x, by_y = swap(mine, "img", 1), swap(mine, "img", 2)
        far_a = swap(by_y[:cut], "img", 1)
        far_b = swap(by_x[cut:], "img", 2)
        after = (by_x, by_y)
        got = [(mine, 0, 0), (by_x, 1, 0), (by_y, 2, 0), (far_a, 3, 0), (far_b, 3, cut)]
        places = [(0, rel, at, shard) for _, rel, at in got] + [(1, rel, at, shard) for _, rel, at in got]
        pieces = [p for p, _, _ in got] + [theirs] + [swap(p, "sp", 1) for p, _, _ in got[1:]]
        gathered.append((pieces, places))

    feats = []
    for (off, width), (pieces, places) in zip(cuts_of(full), gathered):
        key, val, state = project(scal, tok, pieces, places, width, tile)
        feats.append((key, val, sum_tiles(state)))

    prev, grads = [], []
    chunks = cuts_of(full)
    for n, ((off, width), (key, val, state)) in enumerate(zip(chunks, feats)):
        merge = prev if n == len(chunks) - 1 else []
        att, dq, gs = attend(qs, cot, state, off, width, merge, tile)
        prev += [att, dq]
        keep, send = feature_grads(scal, key, val, sum_tiles(gs), float(tok_img), tile)
        grads.append((keep, send))
    attended, d_queries = prev[-2:]

    shards = []
    for keep, send in grads:
        other = swap(send, "sp", 1)
        send_a, send_b, keep_a, keep_b = weight_grads(scal, tok_t, tok_t_other, keep, other, shard, cut)
        a = keep_a + swap(send_a, "img", 1).astype(F32)
        b = keep_b + swap(send_b, "img", 2).astype(F32)
        a0 = a[0] + swap(a[1].astype(BF), "img", 2).astype(F32)
        b0 = b[0] + swap(b[1].astype(BF), "img", 1).astype(F32)
        own = jnp.concatenate([a0, b0], axis=0)
        width = own.shape[1]
        z0, z1 = (spx // 2) % 2, (spx // 4) % 2
        halves = own.reshape(2, shard // 2, width)
        half = lax.dynamic_index_in_dim(halves, z0, 0, False)
        give = lax.dynamic_index_in_dim(halves, 1 - z0, 0, False)
        half = half + swap(give.astype(BF), "sp", 2).astype(F32)
        quarters = half.reshape(2, shard // 4, width)
        quarter = lax.dynamic_index_in_dim(quarters, z1, 0, False)
        give = lax.dynamic_index_in_dim(quarters, 1 - z1, 0, False)
        quarter = (quarter + swap(give.astype(BF), "sp", 4).astype(F32)) * scale
        quarter = quarter.astype(BF)
        back = swap(quarter, "sp", 4)
        low = z1 == 0
        half = jnp.concatenate([jnp.where(low, quarter, back), jnp.where(low, back, quarter)], axis=0)
        back = swap(half, "sp", 2)
        low = z0 == 0
        whole = jnp.concatenate([jnp.where(low, half, back), jnp.where(low, back, half)], axis=0)
        shards.append((whole, swap(whole, "sp", 1)))
    d_tokens = input_grads(
        scal,
        [g for pair in grads for g in pair],
        [p for pieces, _ in gathered for p in pieces],
        [(places, None) for _, places in gathered],
        depth,
        tile,
    )
    mine = jnp.concatenate([m for m, _ in shards], axis=1).astype(F32)
    theirs = jnp.concatenate([t for _, t in shards], axis=1).astype(F32)
    d_w_key = jnp.where(first, mine, theirs)
    d_w_value = jnp.where(first, theirs, mine)
    return attended[None], d_tokens[None], d_queries[None], d_w_key, d_w_value


def body_general(tokens, queries, w_key, w_value, cotangent):
    tok, qs, cot = tokens[0], queries[0], cotangent[0]
    count, depth = tok.shape
    full = w_key.shape[1]
    tile = tile_of(count)
    scal = jnp.zeros((2,), jnp.int32)
    tok_img = count * lax.axis_size("sp")
    scale = 1.0 / (lax.axis_size("img") * tok_img) ** 0.5
    pieces = [lax.all_gather(w, "img", axis=0, tiled=True) for w in (w_key, w_value)]
    places = [(0, None, 0, depth), (1, None, 0, depth)]
    key, val, state = project(scal, tok, pieces, places, full, tile)
    attended, d_queries, gs = attend(qs, cot, lax.psum(state, "sp"), 0, full, [], tile)
    d_key, d_value = feature_grads(scal, key, val, lax.psum(gs, "sp"), float(tok_img), tile)
    d_tokens = input_grads(scal, [d_key, d_value], pieces, [(places, None)], depth, tile)
    out = []
    for d in (d_key, d_value):
        part = lax.psum_scatter(dot(tok, d, 0, 0), "img", scatter_dimension=0, tiled=True)
        out.append(lax.psum(part, "sp") * scale)
    return attended[None], d_tokens[None], d_queries[None], *out


def solution(mesh):
    in_specs = (
        P("img", "sp", None),
        P("img", "sp", None),
        P("img", None),
        P("img", None),
        P("img", "sp", None),
    )
    out_specs = (
        P("img", "sp", None),
        P("img", "sp", None),
        P("img", "sp", None),
        P("img", None),
        P("img", None),
    )
    cubes = mesh.shape["img"] == 4 and mesh.shape["sp"] == 8
    body = body_exchange if cubes else body_general
    return jax.shard_map(body, mesh=mesh, in_specs=in_specs, out_specs=out_specs, check_vma=False)
```

```python
import functools

import jax
import jax.numpy as jnp
from jax import lax
from jax.experimental import pallas as pl
from jax.experimental.pallas import tpu as pltpu
from jax.sharding import PartitionSpec as P

HD = 32
EPS_DEN = 1e-06
LANES = 256
BF, F32 = jnp.bfloat16, jnp.float32
MIB = 1024 * 1024


def dot(a, b, ca, cb):
    return lax.dot_general(a, b, (((ca,), (cb,)), ((), ())), preferred_element_type=F32)


def tiles_of(width):
    return [(s, min(LANES, width - s)) for s in range(0, width, LANES)]


def same_head(w):
    row = lax.broadcasted_iota(jnp.int32, (w, w), 0) // HD
    col = lax.broadcasted_iota(jnp.int32, (w, w), 1) // HD
    return row == col


def diagonal(w):
    return lax.broadcasted_iota(jnp.int32, (w, w), 0) == lax.broadcasted_iota(jnp.int32, (w, w), 1)


def fold(full, w):
    kept = jnp.where(same_head(w), full, 0.0)
    total = kept[0:HD]
    for at in range(HD, w, HD):
        total = total + kept[at : at + HD]
    return total


def unfold(rows, w):
    return jnp.where(same_head(w), jnp.concatenate([rows] * (w // HD), axis=0), 0.0)


def padded(width):
    return -(-width // 128) * 128


def split(x):
    high = x.astype(BF)
    return high, (x - high.astype(F32)).astype(BF)


def call(
    kernel, name, flops, nbytes, args, *, grid, in_specs, out_specs, out_shape, scalars=0, scratch=(), wait=(), vmem=40
):
    at, skip = scalars + len(in_specs), len(wait)

    def run(*refs):
        kernel(*refs[:at], *refs[at + skip :])

    return pl.pallas_call(
        run,
        grid_spec=pltpu.PrefetchScalarGridSpec(
            num_scalar_prefetch=scalars,
            grid=grid,
            in_specs=list(in_specs) + [pl.BlockSpec(memory_space=pltpu.HBM)] * skip,
            out_specs=out_specs,
            scratch_shapes=list(scratch),
        ),
        out_shape=out_shape,
        compiler_params=pltpu.CompilerParams(
            vmem_limit_bytes=vmem * MIB, dimension_semantics=("arbitrary",)
        ),
        cost_estimate=pl.CostEstimate(flops=flops, bytes_accessed=nbytes, transcendentals=0),
        name=name,
    )(*args, *wait)


def place(core, refs, spots, shard, buf, sems):
    span = span_of(shard)
    copies = []
    for n, (ref, (owner, whose, at)) in enumerate(zip(refs, spots)):
        size, skip, off = ref.shape[0], 0, at
        if whose is not None and whose != core:
            skip = 2 * span - shard if at == 0 else 0
            off = shard - span + at + skip
        copies.append(
            pltpu.make_async_copy(
                ref.at[pl.ds(skip, size - skip), :],
                buf.at[pl.ds(owner * shard + off, size - skip), :],
                sems.at[n],
            )
        )
    return copies


def span_of(shard):
    return (shard // 2 + 15) // 16 * 16


def fetch(scal, refs, spots, shard, buf, sems):
    for core in (0, 1):

        @pl.when(scal[0] == core)
        def _():
            copies = place(core, refs, spots, shard, buf, sems)
            for c in copies:
                c.start()
            for c in copies:
                c.wait()


def layout_kernel(scal, block, near, far, give):
    step = pl.program_id(0)
    shard = far.shape[1]
    half = shard // 2
    give[0] = jnp.where(scal[0] == 0, block[0, half:], block[0, :half])
    for r in range(near.shape[1] // shard):

        @pl.when(step == r)
        def _():
            near[:, r * shard : (r + 1) * shard] = block[0].T

    @pl.when(step == pl.num_programs(0) - 1)
    def _():
        far[...] = block[0].T


def token_rows(scal, blocks):
    owners, shard, count = blocks.shape
    wide = (owners - 1) * shard
    return call(
        layout_kernel,
        "token_rows",
        0,
        6 * owners * shard * count,
        (scal, blocks),
        scalars=1,
        grid=(owners,),
        in_specs=[pl.BlockSpec((1, shard, count), lambda i, s: (s[1] ^ i, 0, 0))],
        out_specs=[
            pl.BlockSpec((count, wide), lambda i, s: (0, 0)),
            pl.BlockSpec((count, shard), lambda i, s: (0, 0)),
            pl.BlockSpec((1, shard // 2, count), lambda i, s: (i, 0, 0)),
        ],
        out_shape=[
            jax.ShapeDtypeStruct((count, wide), BF),
            jax.ShapeDtypeStruct((count, shard), BF),
            jax.ShapeDtypeStruct((owners, shard // 2, count), BF),
        ],
    )


def first_kernel(spots, shard, scal, tok, *refs):
    pieces = refs[: len(spots)]
    out, buf, sems = refs[len(spots) :]

    @pl.when(pl.program_id(0) == 0)
    def _():
        fetch(scal, pieces, spots, shard, buf, sems)

    out[...] = dot(tok[...], buf[...], 1, 0)


def key_kernel(spots, shard, scal, tok, part, *refs):
    pieces = refs[: len(spots)]
    k_out, kn_out, buf, sems = refs[len(spots) :]

    @pl.when(pl.program_id(0) == 0)
    def _():
        fetch(scal, pieces, spots, shard, buf, sems)
        kn_out[...] = jnp.zeros_like(kn_out)

    key = jnp.maximum(dot(tok[...], buf[...], 1, 0) + part[...], 0.0).astype(BF)
    k_out[:, : key.shape[1]] = key
    kn_out[...] += jnp.sum(key.astype(F32), axis=0, keepdims=True)


def val_kernel(spots, shard, scal, tok, part, k_ref, *refs):
    pieces = refs[: len(spots)]
    v_out, kv_out, buf, sems = refs[len(spots) :]

    @pl.when(pl.program_id(0) == 0)
    def _():
        fetch(scal, pieces, spots, shard, buf, sems)
        kv_out[...] = jnp.zeros_like(kv_out)

    width = buf.shape[1]
    v_out[:, :width] = (dot(tok[...], buf[...], 1, 0) + part[...]).astype(BF)
    for s, w in tiles_of(width):
        cols = slice(s, s + w)
        kv_out[:, cols] += fold(dot(v_out[:, cols], k_ref[:, cols], 0, 0), w)


def project(kernel, name, scal, tok, feats, pieces, spots, shard, state_rows, tile, wait=()):
    count, depth = tok.shape
    width = pieces[0].shape[1]
    rows = lambda w: pl.BlockSpec((tile, w), lambda i, s: (i, 0))
    kind, wide = (BF, padded(width)) if state_rows else (F32, width)
    return call(
        functools.partial(kernel, spots, shard),
        name,
        2 * count * depth * width,
        2 * (count * depth + depth * width + 3 * count * width),
        (scal, tok, *feats, *pieces),
        scalars=1,
        grid=(count // tile,),
        in_specs=[pl.BlockSpec((tile, depth), lambda i, s: (i, 0))]
        + [rows(x.shape[1]) for x in feats]
        + [pl.BlockSpec(memory_space=pltpu.HBM)] * len(pieces),
        out_specs=[rows(wide)] + [pl.BlockSpec((state_rows, width), lambda i, s: (0, 0))] * bool(state_rows),
        out_shape=[jax.ShapeDtypeStruct((count, wide), kind)]
        + [jax.ShapeDtypeStruct((state_rows, width), F32)] * bool(state_rows),
        scratch=[pltpu.VMEM((depth, width), BF), pltpu.SemaphoreType.DMA((len(pieces),))],
        wait=wait,
    )


def valid_rows(x, width):
    w = x.shape[0]
    return jnp.where(lax.broadcasted_iota(jnp.int32, (w, 1), 0) < width - pl.program_id(0) * w, x, 0)


def valid_lanes(x, width):
    w = x.shape[1]
    return jnp.where(lax.broadcasted_iota(jnp.int32, (1, w), 1) < width - pl.program_id(0) * w, x, 0)


def denominators(q, kn_row, w):
    high, low = split(jnp.where(same_head(w), jnp.broadcast_to(kn_row, (w, w)), 0.0))
    return 1.0 / (dot(high, q, 1, 0) + dot(low, q, 1, 0) + EPS_DEN)


def grad_kernel(width, q_ref, g_ref, kn, gs_out):
    w = q_ref.shape[0]
    q = valid_rows(jnp.maximum(q_ref[...], 0), width)
    g = valid_rows(g_ref[...], width).astype(F32)
    kn_row = valid_lanes(kn[...], width)
    dn = (g * denominators(q, kn_row, w)).astype(BF)
    gs_out[...] = fold(dot(dn, q, 1, 1), w)


def norm_kernel(width, q_ref, g_ref, kn, st, gn_out):
    w = q_ref.shape[0]
    q = valid_rows(jnp.maximum(q_ref[...], 0), width)
    g = valid_rows(g_ref[...], width).astype(F32)
    kn_row = valid_lanes(kn[...], width)
    kv_hi, kv_lo = split(unfold(valid_lanes(st[...], width), w))
    ones = jnp.where(same_head(w), 1.0, 0.0).astype(BF)
    inv = denominators(q, kn_row, w)
    attn = (dot(kv_hi, q, 1, 0) + dot(kv_lo, q, 1, 0)) * inv
    dden = -dot(ones, (g * attn).astype(BF), 1, 0) * inv
    gn = jnp.sum(dden * q.astype(F32), axis=1, keepdims=True)
    gn_out[...] = jnp.sum(jnp.where(diagonal(w), gn, 0.0), axis=0, keepdims=True)


def attend_kernel(width, q_ref, g_ref, kn, st, att_out, dq_out):
    w = q_ref.shape[0]
    q = valid_rows(jnp.maximum(q_ref[...], 0), width)
    g = valid_rows(g_ref[...], width).astype(F32)
    kn_row = valid_lanes(kn[...], width)
    kv = unfold(valid_lanes(st[...], width), w)
    kv_hi, kv_lo = split(kv)
    back_hi, back_lo = split(kv.T)
    kn_col = jnp.sum(jnp.where(diagonal(w), kn_row, 0.0), axis=1, keepdims=True)
    ones = jnp.where(same_head(w), 1.0, 0.0).astype(BF)

    inv = denominators(q, kn_row, w)
    attn = (dot(kv_hi, q, 1, 0) + dot(kv_lo, q, 1, 0)) * inv
    att_out[...] = attn.astype(BF)
    ga_hi, ga_lo = split(g * attn)
    dden = -(dot(ones, ga_hi, 1, 0) + dot(ones, ga_lo, 1, 0)) * inv
    dn_hi, dn_lo = split(g * inv)
    df = dot(back_hi, dn_hi, 1, 0) + dot(back_lo, dn_hi, 1, 0) + dot(back_hi, dn_lo, 1, 0)
    df = df + dden * kn_col
    dq_out[...] = jnp.where(q.astype(F32) > 0, df, 0.0).astype(BF)


def attention(kernel, name, queries, cotangent, states, n_big, state_rows, passes, wait=()):
    full, count = queries.shape
    row = pl.BlockSpec((LANES, count), lambda i: (i, 0))
    state = lambda r: pl.BlockSpec((r, LANES), lambda i: (0, i))
    return call(
        functools.partial(kernel, full),
        name,
        2 * passes * count * full * LANES,
        2 * (2 + n_big) * count * full,
        (queries, cotangent, *states),
        grid=(-(-full // LANES),),
        in_specs=[row, row] + [state(x.shape[0]) for x in states],
        out_specs=[row] * n_big + [state(state_rows)] * bool(state_rows),
        out_shape=[jax.ShapeDtypeStruct((full, count), BF)] * n_big
        + [jax.ShapeDtypeStruct((state_rows, full), F32)] * bool(state_rows),
        wait=wait,
    )


def dval_of(feats, states, scale, high, low, cols):
    (key,) = feats
    return dot(key[:, cols], high, 1, 1) + dot(key[:, cols], low, 1, 1)


def dkey_of(feats, states, scale, high, low, cols):
    key, val = feats
    d = dot(val[:, cols], high, 1, 0) + dot(val[:, cols], low, 1, 0) + states[1][:, cols] * scale
    return jnp.where(key[:, cols].astype(F32) > 0, d, 0.0)


def feature_grad(make, scale, feats, states, out):
    for s, w in tiles_of(states[0].shape[1]):
        cols = slice(s, s + w)
        high, low = split(unfold(states[0][:, cols] * scale, w))
        out[:, cols] = make(feats, states, scale, high, low, cols).astype(BF)


def feature_kernel(make, scale, n_feats, *refs):
    feature_grad(make, scale, refs[:n_feats], refs[n_feats:-1], refs[-1])


def feature_grads(make, name, feats, states, scale):
    count, wide = feats[0].shape
    return call(
        functools.partial(feature_kernel, make, scale, len(feats)),
        name,
        4 * count * wide * LANES,
        2 * count * wide * (1 + len(feats)),
        (*feats, *states),
        grid=(1,),
        in_specs=[pl.BlockSpec(x.shape, lambda i: (0, 0)) for x in (*feats, *states)],
        out_specs=[pl.BlockSpec((count, wide), lambda i: (0, 0))],
        out_shape=[jax.ShapeDtypeStruct((count, wide), BF)],
    )


def weight_kernel(make, scale, n_feats, n_states, scal, t_own, t_other, *refs):
    own, other = refs[:n_feats], refs[n_feats : 2 * n_feats]
    states = refs[2 * n_feats : 2 * n_feats + n_states]
    d_own, send_a, send_b, keep_a, keep_b, d_other = refs[2 * n_feats + n_states :]
    step = pl.program_id(0)

    @pl.when(step == 0)
    def _():
        feature_grad(make, scale, own, states, d_own)
        feature_grad(make, scale, other, states, d_other)

    cut, width = send_a.shape[1:]
    part = dot(t_own[0], d_own[:, :width], 1, 0) + dot(t_other[0], d_other[:, :width], 1, 0)
    a, b = part[:cut], part[cut:]

    @pl.when(step == 0)
    def _():
        send_a[1] = a.astype(BF)
        send_b[1] = b.astype(BF)

    @pl.when(step == 1)
    def _():
        send_b[0] = b.astype(BF)
        keep_a[1] = a

    @pl.when(step == 2)
    def _():
        send_a[0] = a.astype(BF)
        keep_b[1] = b

    @pl.when(step == 3)
    def _():
        keep_a[0] = a
        keep_b[0] = b


def weight_grads(make, name, scal, t_own, t_other, own, other, states, scale, wait=()):
    blocks, rows, count = t_other.shape
    wide, width = own[0].shape[1], states[0].shape[1]
    owned = pl.BlockSpec((1, rows, count), lambda i, s: (2 * (s[1] ^ (3 - i)) + s[0], 0, 0))
    others = pl.BlockSpec((1, rows, count), lambda i, s: (3 - i, 0, 0))
    whole = lambda x: pl.BlockSpec(x.shape, lambda i, s: (0, 0))
    full = lambda r: pl.BlockSpec((2, r, width), lambda i, s: (0, 0, 0))
    cut = (rows // 2 + 15) // 16 * 16
    rest = rows - cut
    return call(
        functools.partial(weight_kernel, make, scale, len(own), len(states)),
        name,
        4 * count * blocks * rows * width,
        4 * count * (blocks * rows + width * len(own)) + 3 * blocks * rows * width,
        (scal, t_own, t_other, *own, *other, *states),
        scalars=1,
        grid=(blocks,),
        in_specs=[owned, others] + [whole(x) for x in (*own, *other, *states)],
        out_specs=[whole(own[0]), full(cut), full(rest), full(cut), full(rest)],
        out_shape=[
            jax.ShapeDtypeStruct((count, wide), BF),
            jax.ShapeDtypeStruct((2, cut, width), BF),
            jax.ShapeDtypeStruct((2, rest, width), BF),
            jax.ShapeDtypeStruct((2, cut, width), F32),
            jax.ShapeDtypeStruct((2, rest, width), F32),
        ],
        scratch=[pltpu.VMEM((count, wide), BF)],
        wait=wait,
        vmem=48,
    )


def input_kernel(counts, spots, shard, scal, d_key, d_val, *refs):
    n = len(spots)
    keys, vals = refs[:n], refs[n : 2 * n]
    out, buf_k, buf_v, sems = refs[2 * n :]
    step = pl.program_id(0)

    def copies(core, k):
        at = sum(counts[:k])
        some = slice(at, at + counts[k])
        return [
            c
            for w, (pieces, buf) in enumerate(((keys, buf_k), (vals, buf_v)))
            for c in place(core, pieces[some], spots[some], shard, buf.at[k], sems.at[w, pl.ds(at, counts[k])])
        ]

    for core in (0, 1):

        @pl.when((scal[0] == core) & (step == 0))
        def _():
            for k in range(len(counts)):
                for c in copies(core, k):
                    c.start()

        for k in range(len(counts)):

            @pl.when((scal[0] == core) & (step == k))
            def _():
                for c in copies(core, k):
                    c.wait()

    width = buf_k.shape[2]
    total = dot(buf_k[step], d_key[:, :width], 1, 1) + dot(buf_v[step], d_val[:, :width], 1, 1)
    out[...] = total.astype(BF)


def input_grads(scal, d_key, d_val, keys, vals, spots, shard, depth, wait=()):
    count, width = d_key.shape[0], keys[0].shape[1]
    owners = depth // shard
    counts = tuple(sum(p[0] == k for p in spots) for k in range(owners))
    local = tuple((0,) + p[1:] for p in spots)
    whole = pl.BlockSpec(d_key.shape, lambda i, s: (0, 0))
    return call(
        functools.partial(input_kernel, counts, local, shard),
        "d_tokens",
        4 * count * depth * width,
        2 * depth * (count + 2 * width) + 4 * count * width,
        (scal, d_key, d_val, *keys, *vals),
        scalars=1,
        grid=(owners,),
        in_specs=[whole, whole] + [pl.BlockSpec(memory_space=pltpu.HBM)] * (len(keys) + len(vals)),
        out_specs=pl.BlockSpec((shard, count), lambda i, s: (s[1] ^ i, 0)),
        out_shape=jax.ShapeDtypeStruct((depth, count), BF),
        scratch=[
            pltpu.VMEM((owners, shard, width), BF),
            pltpu.VMEM((owners, shard, width), BF),
            pltpu.SemaphoreType.DMA((2, len(keys))),
        ],
        wait=wait,
        vmem=56,
    )


def swap(x, axis, bit):
    n = lax.axis_size(axis)
    return lax.ppermute(x, axis, [(i, i ^ bit) for i in range(n)])


def tile_of(count, sizes=(448, 128, 64, 32, 16)):
    return next(t for t in sizes if count % t == 0)


def together(*xs):
    return lax.optimization_barrier(xs)


def body_exchange(tokens, queries, w_key, w_value, cotangent):
    tok_t, qs, cot = tokens[0].T, queries[0].T, cotangent[0].T
    depth, count = tok_t.shape
    shard, full = w_key.shape
    tile = tile_of(count)
    img, spx = lax.axis_index("img"), lax.axis_index("sp")
    core, z = spx % 2, spx // 2
    scal = jnp.stack([core, img]).astype(jnp.int32)
    tok_img = count * lax.axis_size("sp")
    feat_scale = float(tok_img)
    scale = 1.0 / (lax.axis_size("img") * tok_img) ** 0.5

    span = span_of(shard)
    near = span // 32 * 16

    def near_rows(w):
        return jnp.where(core == 0, w[:span], w[shard - span :])

    def gather_near(own):
        return swap(own, "img", 1), swap(own, "img", 2)

    def gather_far(by_x, by_y):
        return swap(by_y[:near], "img", 1), swap(by_x[near:], "img", 2)

    def with_other(*pieces):
        return [p for piece in pieces for p in (piece, swap(piece, "sp", 1))]

    near_spots = ((0, None, 0), (1, 0, 0), (1, 1, 0), (2, 0, 0), (2, 1, 0))
    far_spots = ((0, 0, 0), (0, 1, 0), (0, 0, near), (0, 1, near))
    spots = near_spots + tuple((3,) + p[1:] for p in far_spots)

    def add(x, bit):
        return x + swap(x, "sp", bit)

    def add_beside(x, bit, *beside):
        got, *beside = together(swap(x.astype(BF), "sp", bit), *beside)
        return (x + got.astype(F32), *beside)

    kx, ky = gather_near(near_rows(w_key))
    t_own = tok_t.reshape(2 * lax.axis_size("img"), shard // 2, count)
    tok_near, tok_far, t_give = token_rows(scal, tok_t.reshape(lax.axis_size("img"), shard, count))
    kx, ky, tok_near, tok_far, t_give = together(kx, ky, tok_near, tok_far, t_give)
    kfa, kfb = gather_far(kx, ky)
    keys_near = [w_key] + with_other(kx, ky)
    t_other = swap(t_give, "sp", 1)
    (k_part,) = project(first_kernel, "key_near", scal, tok_near, [], keys_near, near_spots, shard, 0, tile)
    kfa, kfb, k_part, v_own, t_other = together(kfa, kfb, k_part, near_rows(w_value), t_other)
    keys_far = with_other(kfa, kfb)
    vx, vy = gather_near(v_own)
    key, kn = project(key_kernel, "key_feat", scal, tok_far, [k_part], keys_far, far_spots, shard, 1, tile)
    kn, key = together(add(kn, 1), key)
    key_other = swap(key, "sp", 1)
    kn, vx, vy = together(add(add(kn, 2), 4), vx, vy)
    (gs,) = attention(grad_kernel, "grad_state", qs, cot, [kn], 0, HD, 4)
    vx, vy, gs = together(vx, vy, gs)
    vfa, vfb = gather_far(vx, vy)
    gs = add(gs, 1)
    vals_near = [w_value] + with_other(vx, vy)
    (v_part,) = project(
        first_kernel, "val_near", scal, tok_near, [], vals_near, near_spots, shard, 0, tile, [gs]
    )
    gs, v_part, vfa, vfb, key_other = add_beside(gs, 2, v_part, vfa, vfb, key_other)
    vals_far = with_other(vfa, vfb)
    val, kv = project(val_kernel, "val_feat", scal, tok_far, [v_part, key], vals_far, far_spots, shard, HD, tile)
    gs, val, kv = add_beside(gs, 4, val, kv)
    kv, val = together(add(kv, 1), val)
    val_other = swap(val, "sp", 1)

    def reduce_near(parts):
        send_a, send_b, keep_a, keep_b = parts
        return swap(send_a, "img", 1), swap(send_b, "img", 2), keep_a, keep_b

    def add_near(got_a, got_b, keep_a, keep_b):
        a, b = keep_a + got_a.astype(F32), keep_b + got_b.astype(F32)
        return a[0], b[0], a[1].astype(BF), b[1].astype(BF)

    def reduce_far(a, b, send_a, send_b):
        return a, b, swap(send_a, "img", 2), swap(send_b, "img", 1)

    def merge(a, b, ra, rb):
        rows = [a + ra.astype(F32), b + rb.astype(F32)]
        spare = jnp.zeros((-(shard // 2) % 32, full), F32)
        return jnp.concatenate(rows + [spare], axis=0)

    def reduce_z(own):
        quarters = own.reshape(4, own.shape[0] // 4, full)
        pick = lambda k: lax.dynamic_index_in_dim(quarters, z ^ k, 0, False)
        sends = [pick(k).astype(BF) for k in (1, 2, 3)]
        return pick(0), sends, [swap(x, "sp", 2 * k) for k, x in zip((1, 2, 3), sends)]

    def spread_z(mine, gots):
        for got in gots:
            mine = mine + got.astype(F32)
        mine = (mine * scale).astype(BF)
        return [mine] + [swap(mine, "sp", 2 * k) for k in (1, 2, 3)]

    z0, z1 = z % 2, z // 2

    def part_of(x, at):
        return lax.dynamic_index_in_dim(x.reshape(2, x.shape[0] // 2, full), at, 0, False)

    def joined(mine, other, bit):
        low = bit == 0
        return jnp.concatenate([jnp.where(low, mine, other), jnp.where(low, other, mine)], axis=0)

    def ordered(quarters):
        stack = jnp.stack(quarters)
        return jnp.concatenate([lax.dynamic_index_in_dim(stack, z ^ k, 0, False) for k in range(4)], axis=0)

    def assemble(own):
        own = own[: shard // 2]
        other = swap(own, "sp", 1)
        out = jnp.concatenate(
            [jnp.where(core == 0, own, other), jnp.where(core == 0, other, own)], axis=0
        )
        return out.astype(F32)

    gots = [swap(kv.astype(BF), "sp", 2 * k) for k in (1, 2, 3)]
    d_val, *parts_v = weight_grads(
        dval_of, "d_w_value", scal, t_own, t_other, [key], [key_other], [gs], feat_scale, [kv]
    )
    *gots, val_other, d_val, p0, p1, p2, p3 = together(*gots, val_other, d_val, *parts_v)
    parts_v = [p0, p1, p2, p3]
    for got in gots:
        kv = kv + got.astype(F32)
    near_v = reduce_near(parts_v)
    (gn,) = attention(norm_kernel, "grad_norm", qs, cot, [kn, kv], 0, 1, 5)
    gn = add(add(add(gn, 1), 2), 4)
    n0, n1, n2, n3, gn = together(*near_v, gn)
    half_v = add_near(n0, n1, n2, n3)
    d_key, *parts_k = weight_grads(
        dkey_of, "d_w_key", scal, t_own, t_other, [key, val], [key_other, val_other], [gs, gn], feat_scale,
        half_v[2:],
    )
    near_k = reduce_near(parts_k)
    far_v = reduce_far(*half_v)
    own_v = merge(*far_v)
    attended, d_queries = attention(
        attend_kernel, "attend", qs, cot, [kn, kv], 2, 0, 11, [half_v[2], half_v[3]]
    )
    *near_k, attended = together(*near_k, attended)
    half_k = add_near(*near_k)
    far_k = reduce_far(*half_k)
    half_z = part_of(own_v, z0)
    got_v = swap(part_of(own_v, 1 - z0).astype(BF), "sp", 2)
    *far_k, got_v = together(*far_k, got_v)
    mine_k, sends_k, gots_k = reduce_z(merge(*far_k))
    got_v, *sends = together(got_v, *sends_k)
    half_z = half_z + got_v.astype(F32)
    give_v = part_of(half_z, 1 - z1).astype(BF)
    got_v = swap(give_v, "sp", 4)
    d_tokens = input_grads(
        scal, d_key, d_val, keys_near + keys_far, vals_near + vals_far, spots, shard, depth, sends + [give_v]
    )
    *gots_k, d_tokens, got_v = together(*gots_k, d_tokens, got_v)
    quart_k = spread_z(mine_k, gots_k)
    quart_v = ((part_of(half_z, z1) + got_v.astype(F32)) * scale).astype(BF)
    half_v = joined(quart_v, swap(quart_v, "sp", 4), z1)
    whole_v = joined(half_v, swap(half_v, "sp", 2), z0)
    d_w_value = assemble(whole_v)
    d_w_key = assemble(ordered(quart_k))
    return attended.T[None], d_tokens.T[None], d_queries.T[None], d_w_key, d_w_value


def body_general(tokens, queries, w_key, w_value, cotangent):
    tok, qs, cot = tokens[0], queries[0].T, cotangent[0].T
    count = tok.shape[0]
    full = w_key.shape[1]
    tile = tile_of(count)
    tok_img = count * lax.axis_size("sp")
    feat_scale = float(tok_img)
    scale = 1.0 / (lax.axis_size("img") * tok_img) ** 0.5
    keys, vals = (lax.all_gather(w, "img", axis=0, tiled=True) for w in (w_key, w_value))
    key = jnp.maximum(dot(tok, keys, 1, 0), 0.0).astype(BF)
    val = dot(tok, vals, 1, 0).astype(BF)
    by_head = (count, full // HD, HD)
    kv = jnp.einsum("thj,thi->jhi", val.reshape(by_head), key.reshape(by_head), preferred_element_type=F32)
    kv = lax.psum(kv.reshape(HD, full), "sp")
    kn = lax.psum(jnp.sum(key.astype(F32), axis=0, keepdims=True), "sp")
    (gs,) = attention(grad_kernel, "grad_state", qs, cot, [kn], 0, HD, 4)
    gs = lax.psum(gs, "sp")
    (d_val,) = feature_grads(dval_of, "d_value", [key], [gs], feat_scale)
    (gn,) = attention(norm_kernel, "grad_norm", qs, cot, [kn, kv], 0, 1, 5)
    attended, d_queries = attention(attend_kernel, "attend", qs, cot, [kn, kv], 2, 0, 11)
    gn = lax.psum(gn, "sp")
    (d_key,) = feature_grads(dkey_of, "d_key", [key, val], [gs, gn], feat_scale)
    back = [dot(w, d[:, :full], 1, 1) for w, d in ((keys, d_key), (vals, d_val))]
    d_tokens = (back[0] + back[1]).astype(BF)
    out = []
    for d in (d_key, d_val):
        part = lax.psum_scatter(dot(tok, d[:, :full], 0, 0), "img", scatter_dimension=0, tiled=True)
        out.append(lax.psum(part, "sp") * scale)
    return attended.T[None], d_tokens.T[None], d_queries.T[None], *out


def solution(mesh):
    in_specs = (
        P("img", "sp", None),
        P("img", "sp", None),
        P("img", None),
        P("img", None),
        P("img", "sp", None),
    )
    out_specs = (
        P("img", "sp", None),
        P("img", "sp", None),
        P("img", "sp", None),
        P("img", None),
        P("img", None),
    )
    cubes = mesh.shape["img"] == 4 and mesh.shape["sp"] == 8
    body = body_exchange if cubes else body_general
    return jax.shard_map(body, mesh=mesh, in_specs=in_specs, out_specs=out_specs, check_vma=False)
```

```python
import functools

import jax
import jax.numpy as jnp
from jax import lax
from jax.experimental import pallas as pl
from jax.experimental.pallas import tpu as pltpu
from jax.sharding import PartitionSpec as P

HD = 32
EPS_DEN = 1e-06
LANES = 256
BF, F32 = jnp.bfloat16, jnp.float32
MIB = 1024 * 1024


def dot(a, b, ca, cb):
    return lax.dot_general(a, b, (((ca,), (cb,)), ((), ())), preferred_element_type=F32)


def tiles_of(width):
    return [(s, min(LANES, width - s)) for s in range(0, width, LANES)]


def same_head(w):
    row = lax.broadcasted_iota(jnp.int32, (w, w), 0) // HD
    col = lax.broadcasted_iota(jnp.int32, (w, w), 1) // HD
    return row == col


def diagonal(w):
    return lax.broadcasted_iota(jnp.int32, (w, w), 0) == lax.broadcasted_iota(jnp.int32, (w, w), 1)


def fold(full, w):
    kept = jnp.where(same_head(w), full, 0.0)
    total = kept[0:HD]
    for at in range(HD, w, HD):
        total = total + kept[at : at + HD]
    return total


def unfold(rows, w):
    return jnp.where(same_head(w), jnp.concatenate([rows] * (w // HD), axis=0), 0.0)


def padded(width):
    return -(-width // 128) * 128


def split(x):
    high = x.astype(BF)
    return high, (x - high.astype(F32)).astype(BF)


def call(
    kernel, name, flops, nbytes, args, *, grid, in_specs, out_specs, out_shape, scalars=0, scratch=(), wait=(), vmem=40
):
    at, skip = scalars + len(in_specs), len(wait)

    def run(*refs):
        kernel(*refs[:at], *refs[at + skip :])

    return pl.pallas_call(
        run,
        grid_spec=pltpu.PrefetchScalarGridSpec(
            num_scalar_prefetch=scalars,
            grid=grid,
            in_specs=list(in_specs) + [pl.BlockSpec(memory_space=pltpu.HBM)] * skip,
            out_specs=out_specs,
            scratch_shapes=list(scratch),
        ),
        out_shape=out_shape,
        compiler_params=pltpu.CompilerParams(
            vmem_limit_bytes=vmem * MIB, dimension_semantics=("arbitrary",)
        ),
        cost_estimate=pl.CostEstimate(flops=flops, bytes_accessed=nbytes, transcendentals=0),
        name=name,
    )(*args, *wait)


def place(core, refs, spots, shard, buf, sems):
    span = span_of(shard)
    copies = []
    for n, (ref, (owner, whose, at)) in enumerate(zip(refs, spots)):
        size, skip, off = ref.shape[0], 0, at
        if whose is not None and whose != core:
            skip = 2 * span - shard if at == 0 else 0
            off = shard - span + at + skip
        copies.append(
            pltpu.make_async_copy(
                ref.at[pl.ds(skip, size - skip), :],
                buf.at[pl.ds(owner * shard + off, size - skip), :],
                sems.at[n],
            )
        )
    return copies


def span_of(shard):
    return (shard // 2 + 15) // 16 * 16


def fetch(scal, refs, spots, shard, buf, sems):
    for core in (0, 1):

        @pl.when(scal[0] == core)
        def _():
            copies = place(core, refs, spots, shard, buf, sems)
            for c in copies:
                c.start()
            for c in copies:
                c.wait()


def layout_kernel(scal, block, near, far, give):
    step = pl.program_id(0)
    shard = far.shape[1]
    half = shard // 2
    give[0] = jnp.where(scal[0] == 0, block[0, half:], block[0, :half])
    for r in range(near.shape[1] // shard):

        @pl.when(step == r)
        def _():
            near[:, r * shard : (r + 1) * shard] = block[0].T

    @pl.when(step == pl.num_programs(0) - 1)
    def _():
        far[...] = block[0].T


def token_rows(scal, blocks):
    owners, shard, count = blocks.shape
    wide = (owners - 1) * shard
    return call(
        layout_kernel,
        "token_rows",
        0,
        6 * owners * shard * count,
        (scal, blocks),
        scalars=1,
        grid=(owners,),
        in_specs=[pl.BlockSpec((1, shard, count), lambda i, s: (s[1] ^ i, 0, 0))],
        out_specs=[
            pl.BlockSpec((count, wide), lambda i, s: (0, 0)),
            pl.BlockSpec((count, shard), lambda i, s: (0, 0)),
            pl.BlockSpec((1, shard // 2, count), lambda i, s: (i, 0, 0)),
        ],
        out_shape=[
            jax.ShapeDtypeStruct((count, wide), BF),
            jax.ShapeDtypeStruct((count, shard), BF),
            jax.ShapeDtypeStruct((owners, shard // 2, count), BF),
        ],
    )


def first_kernel(spots, shard, scal, tok, *refs):
    pieces = refs[: len(spots)]
    out, buf, sems = refs[len(spots) :]

    @pl.when(pl.program_id(0) == 0)
    def _():
        fetch(scal, pieces, spots, shard, buf, sems)

    out[...] = dot(tok[...], buf[...], 1, 0)


def key_kernel(spots, shard, scal, tok, part, *refs):
    pieces = refs[: len(spots)]
    k_out, kn_out, buf, sems = refs[len(spots) :]

    @pl.when(pl.program_id(0) == 0)
    def _():
        fetch(scal, pieces, spots, shard, buf, sems)
        kn_out[...] = jnp.zeros_like(kn_out)

    key = jnp.maximum(dot(tok[...], buf[...], 1, 0) + part[...], 0.0).astype(BF)
    k_out[:, : key.shape[1]] = key
    kn_out[...] += jnp.sum(key.astype(F32), axis=0, keepdims=True)


def val_kernel(spots, shard, scal, tok, part, k_ref, *refs):
    pieces = refs[: len(spots)]
    v_out, kv_out, buf, sems = refs[len(spots) :]

    @pl.when(pl.program_id(0) == 0)
    def _():
        fetch(scal, pieces, spots, shard, buf, sems)
        kv_out[...] = jnp.zeros_like(kv_out)

    width = buf.shape[1]
    v_out[:, :width] = (dot(tok[...], buf[...], 1, 0) + part[...]).astype(BF)
    for s, w in tiles_of(width):
        cols = slice(s, s + w)
        kv_out[:, cols] += fold(dot(v_out[:, cols], k_ref[:, cols], 0, 0), w)


def project(kernel, name, scal, tok, feats, pieces, spots, shard, state_rows, tile, wait=()):
    count, depth = tok.shape
    width = pieces[0].shape[1]
    rows = lambda w: pl.BlockSpec((tile, w), lambda i, s: (i, 0))
    kind, wide = (BF, padded(width)) if state_rows else (F32, width)
    return call(
        functools.partial(kernel, spots, shard),
        name,
        2 * count * depth * width,
        2 * (count * depth + depth * width + 3 * count * width),
        (scal, tok, *feats, *pieces),
        scalars=1,
        grid=(count // tile,),
        in_specs=[pl.BlockSpec((tile, depth), lambda i, s: (i, 0))]
        + [rows(x.shape[1]) for x in feats]
        + [pl.BlockSpec(memory_space=pltpu.HBM)] * len(pieces),
        out_specs=[rows(wide)] + [pl.BlockSpec((state_rows, width), lambda i, s: (0, 0))] * bool(state_rows),
        out_shape=[jax.ShapeDtypeStruct((count, wide), kind)]
        + [jax.ShapeDtypeStruct((state_rows, width), F32)] * bool(state_rows),
        scratch=[pltpu.VMEM((depth, width), BF), pltpu.SemaphoreType.DMA((len(pieces),))],
        wait=wait,
    )


def valid_rows(x, width):
    w = x.shape[0]
    return jnp.where(lax.broadcasted_iota(jnp.int32, (w, 1), 0) < width - pl.program_id(0) * w, x, 0)


def valid_lanes(x, width):
    w = x.shape[1]
    return jnp.where(lax.broadcasted_iota(jnp.int32, (1, w), 1) < width - pl.program_id(0) * w, x, 0)


def denominators(q, kn_row, w):
    high, low = split(jnp.where(same_head(w), jnp.broadcast_to(kn_row, (w, w)), 0.0))
    return 1.0 / (dot(high, q, 1, 0) + dot(low, q, 1, 0) + EPS_DEN)


def grad_kernel(width, q_ref, g_ref, kn, gs_out):
    w = q_ref.shape[0]
    q = valid_rows(jnp.maximum(q_ref[...], 0), width)
    g = valid_rows(g_ref[...], width).astype(F32)
    kn_row = valid_lanes(kn[...], width)
    dn = (g * denominators(q, kn_row, w)).astype(BF)
    gs_out[...] = fold(dot(dn, q, 1, 1), w)


def norm_kernel(width, q_ref, g_ref, kn, st, gn_out):
    w = q_ref.shape[0]
    q = valid_rows(jnp.maximum(q_ref[...], 0), width)
    g = valid_rows(g_ref[...], width).astype(F32)
    kn_row = valid_lanes(kn[...], width)
    kv_hi, kv_lo = split(unfold(valid_lanes(st[...], width), w))
    ones = jnp.where(same_head(w), 1.0, 0.0).astype(BF)
    inv = denominators(q, kn_row, w)
    attn = (dot(kv_hi, q, 1, 0) + dot(kv_lo, q, 1, 0)) * inv
    dden = -dot(ones, (g * attn).astype(BF), 1, 0) * inv
    gn = jnp.sum(dden * q.astype(F32), axis=1, keepdims=True)
    gn_out[...] = jnp.sum(jnp.where(diagonal(w), gn, 0.0), axis=0, keepdims=True)


def attend_kernel(width, q_ref, g_ref, kn, st, att_out, dq_out):
    w = q_ref.shape[0]
    q = valid_rows(jnp.maximum(q_ref[...], 0), width)
    g = valid_rows(g_ref[...], width).astype(F32)
    kn_row = valid_lanes(kn[...], width)
    kv = unfold(valid_lanes(st[...], width), w)
    kv_hi, kv_lo = split(kv)
    back_hi, back_lo = split(kv.T)
    kn_col = jnp.sum(jnp.where(diagonal(w), kn_row, 0.0), axis=1, keepdims=True)
    ones = jnp.where(same_head(w), 1.0, 0.0).astype(BF)

    inv = denominators(q, kn_row, w)
    attn = (dot(kv_hi, q, 1, 0) + dot(kv_lo, q, 1, 0)) * inv
    att_out[...] = attn.astype(BF)
    ga_hi, ga_lo = split(g * attn)
    dden = -(dot(ones, ga_hi, 1, 0) + dot(ones, ga_lo, 1, 0)) * inv
    dn_hi, dn_lo = split(g * inv)
    df = dot(back_hi, dn_hi, 1, 0) + dot(back_lo, dn_hi, 1, 0) + dot(back_hi, dn_lo, 1, 0)
    df = df + dden * kn_col
    dq_out[...] = jnp.where(q.astype(F32) > 0, df, 0.0).astype(BF)


def attention(kernel, name, queries, cotangent, states, n_big, state_rows, passes, wait=()):
    full, count = queries.shape
    row = pl.BlockSpec((LANES, count), lambda i: (i, 0))
    state = lambda r: pl.BlockSpec((r, LANES), lambda i: (0, i))
    return call(
        functools.partial(kernel, full),
        name,
        2 * passes * count * full * LANES,
        2 * (2 + n_big) * count * full,
        (queries, cotangent, *states),
        grid=(-(-full // LANES),),
        in_specs=[row, row] + [state(x.shape[0]) for x in states],
        out_specs=[row] * n_big + [state(state_rows)] * bool(state_rows),
        out_shape=[jax.ShapeDtypeStruct((full, count), BF)] * n_big
        + [jax.ShapeDtypeStruct((state_rows, full), F32)] * bool(state_rows),
        wait=wait,
    )


def dval_of(feats, states, scale, high, low, cols):
    (key,) = feats
    return dot(key[:, cols], high, 1, 1) + dot(key[:, cols], low, 1, 1)


def dkey_of(feats, states, scale, high, low, cols):
    key, val = feats
    d = dot(val[:, cols], high, 1, 0) + dot(val[:, cols], low, 1, 0) + states[1][:, cols] * scale
    return jnp.where(key[:, cols].astype(F32) > 0, d, 0.0)


def feature_grad(make, scale, feats, states, out):
    for s, w in tiles_of(states[0].shape[1]):
        cols = slice(s, s + w)
        high, low = split(unfold(states[0][:, cols] * scale, w))
        out[:, cols] = make(feats, states, scale, high, low, cols).astype(BF)


def feature_kernel(make, scale, n_feats, *refs):
    feature_grad(make, scale, refs[:n_feats], refs[n_feats:-1], refs[-1])


def feature_grads(make, name, feats, states, scale):
    count, wide = feats[0].shape
    return call(
        functools.partial(feature_kernel, make, scale, len(feats)),
        name,
        4 * count * wide * LANES,
        2 * count * wide * (1 + len(feats)),
        (*feats, *states),
        grid=(1,),
        in_specs=[pl.BlockSpec(x.shape, lambda i: (0, 0)) for x in (*feats, *states)],
        out_specs=[pl.BlockSpec((count, wide), lambda i: (0, 0))],
        out_shape=[jax.ShapeDtypeStruct((count, wide), BF)],
    )


def weight_kernel(make, scale, n_feats, n_states, scal, t_own, t_other, *refs):
    own, other = refs[:n_feats], refs[n_feats : 2 * n_feats]
    states = refs[2 * n_feats : 2 * n_feats + n_states]
    d_own, send_a, send_b, keep_a, keep_b, d_other = refs[2 * n_feats + n_states :]
    step = pl.program_id(0)

    @pl.when(step == 0)
    def _():
        feature_grad(make, scale, own, states, d_own)
        feature_grad(make, scale, other, states, d_other)

    cut, width = send_a.shape[1:]
    part = dot(t_own[0], d_own[:, :width], 1, 0) + dot(t_other[0], d_other[:, :width], 1, 0)
    a, b = part[:cut], part[cut:]

    @pl.when(step == 0)
    def _():
        send_a[1] = a.astype(BF)
        send_b[1] = b.astype(BF)

    @pl.when(step == 1)
    def _():
        send_b[0] = b.astype(BF)
        keep_a[1] = a

    @pl.when(step == 2)
    def _():
        send_a[0] = a.astype(BF)
        keep_b[1] = b

    @pl.when(step == 3)
    def _():
        keep_a[0] = a
        keep_b[0] = b


def weight_grads(make, name, scal, t_own, t_other, own, other, states, scale, wait=()):
    blocks, rows, count = t_other.shape
    wide, width = own[0].shape[1], states[0].shape[1]
    owned = pl.BlockSpec((1, rows, count), lambda i, s: (2 * (s[1] ^ (3 - i)) + s[0], 0, 0))
    others = pl.BlockSpec((1, rows, count), lambda i, s: (3 - i, 0, 0))
    whole = lambda x: pl.BlockSpec(x.shape, lambda i, s: (0, 0))
    full = lambda r: pl.BlockSpec((2, r, width), lambda i, s: (0, 0, 0))
    cut = (rows // 2 + 15) // 16 * 16
    rest = rows - cut
    return call(
        functools.partial(weight_kernel, make, scale, len(own), len(states)),
        name,
        4 * count * blocks * rows * width,
        4 * count * (blocks * rows + width * len(own)) + 3 * blocks * rows * width,
        (scal, t_own, t_other, *own, *other, *states),
        scalars=1,
        grid=(blocks,),
        in_specs=[owned, others] + [whole(x) for x in (*own, *other, *states)],
        out_specs=[whole(own[0]), full(cut), full(rest), full(cut), full(rest)],
        out_shape=[
            jax.ShapeDtypeStruct((count, wide), BF),
            jax.ShapeDtypeStruct((2, cut, width), BF),
            jax.ShapeDtypeStruct((2, rest, width), BF),
            jax.ShapeDtypeStruct((2, cut, width), F32),
            jax.ShapeDtypeStruct((2, rest, width), F32),
        ],
        scratch=[pltpu.VMEM((count, wide), BF)],
        wait=wait,
        vmem=48,
    )


def input_kernel(counts, spots, shard, scal, d_key, d_val, *refs):
    n = len(spots)
    keys, vals = refs[:n], refs[n : 2 * n]
    out, buf_k, buf_v, sems = refs[2 * n :]
    step = pl.program_id(0)

    def copies(core, k):
        at = sum(counts[:k])
        some = slice(at, at + counts[k])
        return [
            c
            for w, (pieces, buf) in enumerate(((keys, buf_k), (vals, buf_v)))
            for c in place(core, pieces[some], spots[some], shard, buf.at[k], sems.at[w, pl.ds(at, counts[k])])
        ]

    for core in (0, 1):

        @pl.when((scal[0] == core) & (step == 0))
        def _():
            for k in range(len(counts)):
                for c in copies(core, k):
                    c.start()

        for k in range(len(counts)):

            @pl.when((scal[0] == core) & (step == k))
            def _():
                for c in copies(core, k):
                    c.wait()

    width = buf_k.shape[2]
    total = dot(buf_k[step], d_key[:, :width], 1, 1) + dot(buf_v[step], d_val[:, :width], 1, 1)
    out[...] = total.astype(BF)


def input_grads(scal, d_key, d_val, keys, vals, spots, shard, depth, wait=()):
    count, width = d_key.shape[0], keys[0].shape[1]
    owners = depth // shard
    counts = tuple(sum(p[0] == k for p in spots) for k in range(owners))
    local = tuple((0,) + p[1:] for p in spots)
    whole = pl.BlockSpec(d_key.shape, lambda i, s: (0, 0))
    return call(
        functools.partial(input_kernel, counts, local, shard),
        "d_tokens",
        4 * count * depth * width,
        2 * depth * (count + 2 * width) + 4 * count * width,
        (scal, d_key, d_val, *keys, *vals),
        scalars=1,
        grid=(owners,),
        in_specs=[whole, whole] + [pl.BlockSpec(memory_space=pltpu.HBM)] * (len(keys) + len(vals)),
        out_specs=pl.BlockSpec((shard, count), lambda i, s: (s[1] ^ i, 0)),
        out_shape=jax.ShapeDtypeStruct((depth, count), BF),
        scratch=[
            pltpu.VMEM((owners, shard, width), BF),
            pltpu.VMEM((owners, shard, width), BF),
            pltpu.SemaphoreType.DMA((2, len(keys))),
        ],
        wait=wait,
        vmem=56,
    )


def swap(x, axis, bit):
    n = lax.axis_size(axis)
    return lax.ppermute(x, axis, [(i, i ^ bit) for i in range(n)])


def tile_of(count, sizes=(448, 128, 64, 32, 16)):
    return next(t for t in sizes if count % t == 0)


def together(*xs):
    return lax.optimization_barrier(xs)


def body_exchange(tokens, queries, w_key, w_value, cotangent):
    tok_t, qs, cot = tokens[0].T, queries[0].T, cotangent[0].T
    depth, count = tok_t.shape
    shard, full = w_key.shape
    tile = tile_of(count)
    img, spx = lax.axis_index("img"), lax.axis_index("sp")
    core, z = spx % 2, spx // 2
    scal = jnp.stack([core, img]).astype(jnp.int32)
    tok_img = count * lax.axis_size("sp")
    feat_scale = float(tok_img)
    scale = 1.0 / (lax.axis_size("img") * tok_img) ** 0.5

    span = span_of(shard)
    near = span // 32 * 16

    def near_rows(w):
        return jnp.where(core == 0, w[:span], w[shard - span :])

    def gather_near(own):
        return swap(own, "img", 1), swap(own, "img", 2)

    def gather_far(by_x, by_y):
        return swap(by_y[:near], "img", 1), swap(by_x[near:], "img", 2)

    def with_other(*pieces):
        return [p for piece in pieces for p in (piece, swap(piece, "sp", 1))]

    near_spots = ((0, None, 0), (1, 0, 0), (1, 1, 0), (2, 0, 0), (2, 1, 0))
    far_spots = ((0, 0, 0), (0, 1, 0), (0, 0, near), (0, 1, near))
    spots = near_spots + tuple((3,) + p[1:] for p in far_spots)

    def add(x, bit):
        return x + swap(x, "sp", bit)

    def add_beside(x, bit, *beside):
        got, *beside = together(swap(x.astype(BF), "sp", bit), *beside)
        return (x + got.astype(F32), *beside)

    kx, ky = gather_near(near_rows(w_key))
    t_own = tok_t.reshape(2 * lax.axis_size("img"), shard // 2, count)
    tok_near, tok_far, t_give = token_rows(scal, tok_t.reshape(lax.axis_size("img"), shard, count))
    kx, ky, tok_near, tok_far, t_give = together(kx, ky, tok_near, tok_far, t_give)
    kfa, kfb = gather_far(kx, ky)
    keys_near = [w_key] + with_other(kx, ky)
    t_other = swap(t_give, "sp", 1)
    (k_part,) = project(first_kernel, "key_near", scal, tok_near, [], keys_near, near_spots, shard, 0, tile)
    kfa, kfb, k_part, v_own, t_other = together(kfa, kfb, k_part, near_rows(w_value), t_other)
    keys_far = with_other(kfa, kfb)
    vx, vy = gather_near(v_own)
    key, kn = project(key_kernel, "key_feat", scal, tok_far, [k_part], keys_far, far_spots, shard, 1, tile)
    kn, key = together(add(kn, 1), key)
    key_other = swap(key, "sp", 1)
    kn, vx, vy = together(add(add(kn, 2), 4), vx, vy)
    (gs,) = attention(grad_kernel, "grad_state", qs, cot, [kn], 0, HD, 4)
    vx, vy, gs = together(vx, vy, gs)
    vfa, vfb = gather_far(vx, vy)
    gs = add(gs, 1)
    vals_near = [w_value] + with_other(vx, vy)
    (v_part,) = project(
        first_kernel, "val_near", scal, tok_near, [], vals_near, near_spots, shard, 0, tile, [gs]
    )
    gs, v_part, vfa, vfb, key_other = add_beside(gs, 2, v_part, vfa, vfb, key_other)
    vals_far = with_other(vfa, vfb)
    val, kv = project(val_kernel, "val_feat", scal, tok_far, [v_part, key], vals_far, far_spots, shard, HD, tile)
    gs, val, kv = add_beside(gs, 4, val, kv)
    kv, val = together(add(kv, 1), val)
    val_other = swap(val, "sp", 1)

    def reduce_near(parts):
        send_a, send_b, keep_a, keep_b = parts
        return swap(send_a, "img", 1), swap(send_b, "img", 2), keep_a, keep_b

    def add_near(got_a, got_b, keep_a, keep_b):
        a, b = keep_a + got_a.astype(F32), keep_b + got_b.astype(F32)
        return a[0], b[0], a[1].astype(BF), b[1].astype(BF)

    def reduce_far(a, b, send_a, send_b):
        return a, b, swap(send_a, "img", 2), swap(send_b, "img", 1)

    def merge(a, b, ra, rb):
        rows = [a + ra.astype(F32), b + rb.astype(F32)]
        spare = jnp.zeros((-(shard // 2) % 32, full), F32)
        return jnp.concatenate(rows + [spare], axis=0)

    def reduce_z(own):
        quarters = own.reshape(4, own.shape[0] // 4, full)
        pick = lambda k: lax.dynamic_index_in_dim(quarters, z ^ k, 0, False)
        sends = [pick(k).astype(BF) for k in (1, 2, 3)]
        return pick(0), sends, [swap(x, "sp", 2 * k) for k, x in zip((1, 2, 3), sends)]

    def spread_z(mine, gots):
        for got in gots:
            mine = mine + got.astype(F32)
        mine = (mine * scale).astype(BF)
        return [mine] + [swap(mine, "sp", 2 * k) for k in (1, 2, 3)]

    z0, z1 = z % 2, z // 2

    def part_of(x, at):
        return lax.dynamic_index_in_dim(x.reshape(2, x.shape[0] // 2, full), at, 0, False)

    def joined(mine, other, bit):
        low = bit == 0
        return jnp.concatenate([jnp.where(low, mine, other), jnp.where(low, other, mine)], axis=0)

    def ordered(quarters):
        stack = jnp.stack(quarters)
        return jnp.concatenate([lax.dynamic_index_in_dim(stack, z ^ k, 0, False) for k in range(4)], axis=0)

    def assemble(own):
        own = own[: shard // 2]
        other = swap(own, "sp", 1)
        out = jnp.concatenate(
            [jnp.where(core == 0, own, other), jnp.where(core == 0, other, own)], axis=0
        )
        return out.astype(F32)

    gots = [swap(kv.astype(BF), "sp", 2 * k) for k in (1, 2, 3)]
    d_val, *parts_v = weight_grads(
        dval_of, "d_w_value", scal, t_own, t_other, [key], [key_other], [gs], feat_scale, [kv]
    )
    *gots, val_other, d_val, p0, p1, p2, p3 = together(*gots, val_other, d_val, *parts_v)
    parts_v = [p0, p1, p2, p3]
    for got in gots:
        kv = kv + got.astype(F32)
    near_v = reduce_near(parts_v)
    (gn,) = attention(norm_kernel, "grad_norm", qs, cot, [kn, kv], 0, 1, 5)
    gn = add(add(add(gn, 1), 2), 4)
    n0, n1, n2, n3, gn = together(*near_v, gn)
    half_v = add_near(n0, n1, n2, n3)
    d_key, *parts_k = weight_grads(
        dkey_of, "d_w_key", scal, t_own, t_other, [key, val], [key_other, val_other], [gs, gn], feat_scale,
        half_v[2:],
    )
    near_k = reduce_near(parts_k)
    far_v = reduce_far(*half_v)
    own_v = merge(*far_v)
    attended, d_queries = attention(
        attend_kernel, "attend", qs, cot, [kn, kv], 2, 0, 11, [parts_k[0], parts_k[1]]
    )
    half_z = part_of(own_v, z0)
    got_v = swap(part_of(own_v, 1 - z0).astype(BF), "sp", 2)
    *near_k, attended, got_v = together(*near_k, attended, got_v)
    half_k = add_near(*near_k)
    far_k = reduce_far(*half_k)
    half_z = half_z + got_v.astype(F32)
    got_v = swap(part_of(half_z, 1 - z1).astype(BF), "sp", 4)
    *far_k, got_v = together(*far_k, got_v)
    mine_k, sends_k, gots_k = reduce_z(merge(*far_k))
    quart_v = ((part_of(half_z, z1) + got_v.astype(F32)) * scale).astype(BF)
    got_v = swap(quart_v, "sp", 4)
    d_tokens = input_grads(
        scal, d_key, d_val, keys_near + keys_far, vals_near + vals_far, spots, shard, depth, sends_k + [quart_v]
    )
    *gots_k, d_tokens, got_v = together(*gots_k, d_tokens, got_v)
    quart_k = spread_z(mine_k, gots_k)
    half_v = joined(quart_v, got_v, z1)
    whole_v = joined(half_v, swap(half_v, "sp", 2), z0)
    d_w_value = assemble(whole_v)
    d_w_key = assemble(ordered(quart_k))
    return attended.T[None], d_tokens.T[None], d_queries.T[None], d_w_key, d_w_value


def body_general(tokens, queries, w_key, w_value, cotangent):
    tok, qs, cot = tokens[0], queries[0].T, cotangent[0].T
    count = tok.shape[0]
    full = w_key.shape[1]
    tile = tile_of(count)
    tok_img = count * lax.axis_size("sp")
    feat_scale = float(tok_img)
    scale = 1.0 / (lax.axis_size("img") * tok_img) ** 0.5
    keys, vals = (lax.all_gather(w, "img", axis=0, tiled=True) for w in (w_key, w_value))
    key = jnp.maximum(dot(tok, keys, 1, 0), 0.0).astype(BF)
    val = dot(tok, vals, 1, 0).astype(BF)
    by_head = (count, full // HD, HD)
    kv = jnp.einsum("thj,thi->jhi", val.reshape(by_head), key.reshape(by_head), preferred_element_type=F32)
    kv = lax.psum(kv.reshape(HD, full), "sp")
    kn = lax.psum(jnp.sum(key.astype(F32), axis=0, keepdims=True), "sp")
    (gs,) = attention(grad_kernel, "grad_state", qs, cot, [kn], 0, HD, 4)
    gs = lax.psum(gs, "sp")
    (d_val,) = feature_grads(dval_of, "d_value", [key], [gs], feat_scale)
    (gn,) = attention(norm_kernel, "grad_norm", qs, cot, [kn, kv], 0, 1, 5)
    attended, d_queries = attention(attend_kernel, "attend", qs, cot, [kn, kv], 2, 0, 11)
    gn = lax.psum(gn, "sp")
    (d_key,) = feature_grads(dkey_of, "d_key", [key, val], [gs, gn], feat_scale)
    back = [dot(w, d[:, :full], 1, 1) for w, d in ((keys, d_key), (vals, d_val))]
    d_tokens = (back[0] + back[1]).astype(BF)
    out = []
    for d in (d_key, d_val):
        part = lax.psum_scatter(dot(tok, d[:, :full], 0, 0), "img", scatter_dimension=0, tiled=True)
        out.append(lax.psum(part, "sp") * scale)
    return attended.T[None], d_tokens.T[None], d_queries.T[None], *out


def solution(mesh):
    in_specs = (
        P("img", "sp", None),
        P("img", "sp", None),
        P("img", None),
        P("img", None),
        P("img", "sp", None),
    )
    out_specs = (
        P("img", "sp", None),
        P("img", "sp", None),
        P("img", "sp", None),
        P("img", None),
        P("img", None),
    )
    cubes = mesh.shape["img"] == 4 and mesh.shape["sp"] == 8
    body = body_exchange if cubes else body_general
    return jax.shard_map(body, mesh=mesh, in_specs=in_specs, out_specs=out_specs, check_vma=False)
```

```python
import functools

import jax
import jax.numpy as jnp
from jax import lax
from jax.experimental import pallas as pl
from jax.experimental.pallas import tpu as pltpu
from jax.sharding import PartitionSpec as P

HD = 32
EPS_DEN = 1e-06
LANES = 256
BF, F32 = jnp.bfloat16, jnp.float32
MIB = 1024 * 1024


def dot(a, b, ca, cb):
    return lax.dot_general(a, b, (((ca,), (cb,)), ((), ())), preferred_element_type=F32)


def tiles_of(width):
    return [(s, min(LANES, width - s)) for s in range(0, width, LANES)]


def same_head(w):
    row = lax.broadcasted_iota(jnp.int32, (w, w), 0) // HD
    col = lax.broadcasted_iota(jnp.int32, (w, w), 1) // HD
    return row == col


def diagonal(w):
    return lax.broadcasted_iota(jnp.int32, (w, w), 0) == lax.broadcasted_iota(jnp.int32, (w, w), 1)


def fold(full, w):
    kept = jnp.where(same_head(w), full, 0.0)
    total = kept[0:HD]
    for at in range(HD, w, HD):
        total = total + kept[at : at + HD]
    return total


def unfold(rows, w):
    return jnp.where(same_head(w), jnp.concatenate([rows] * (w // HD), axis=0), 0.0)


def padded(width):
    return -(-width // 128) * 128


def split(x):
    high = x.astype(BF)
    return high, (x - high.astype(F32)).astype(BF)


def call(
    kernel, name, flops, nbytes, args, *, grid, in_specs, out_specs, out_shape, scalars=0, scratch=(), wait=(), vmem=40
):
    at, skip = scalars + len(in_specs), len(wait)

    def run(*refs):
        kernel(*refs[:at], *refs[at + skip :])

    return pl.pallas_call(
        run,
        grid_spec=pltpu.PrefetchScalarGridSpec(
            num_scalar_prefetch=scalars,
            grid=grid,
            in_specs=list(in_specs) + [pl.BlockSpec(memory_space=pltpu.HBM)] * skip,
            out_specs=out_specs,
            scratch_shapes=list(scratch),
        ),
        out_shape=out_shape,
        compiler_params=pltpu.CompilerParams(
            vmem_limit_bytes=vmem * MIB, dimension_semantics=("arbitrary",)
        ),
        cost_estimate=pl.CostEstimate(flops=flops, bytes_accessed=nbytes, transcendentals=0),
        name=name,
    )(*args, *wait)


def place(core, refs, spots, shard, buf, sems):
    span = span_of(shard)
    copies = []
    for n, (ref, (owner, whose, at)) in enumerate(zip(refs, spots)):
        size, skip, off = ref.shape[0], 0, at
        if whose is not None and whose != core:
            skip = 2 * span - shard if at == 0 else 0
            off = shard - span + at + skip
        copies.append(
            pltpu.make_async_copy(
                ref.at[pl.ds(skip, size - skip), :],
                buf.at[pl.ds(owner * shard + off, size - skip), :],
                sems.at[n],
            )
        )
    return copies


def span_of(shard):
    return (shard // 2 + 15) // 16 * 16


def fetch(scal, refs, spots, shard, buf, sems):
    for core in (0, 1):

        @pl.when(scal[0] == core)
        def _():
            copies = place(core, refs, spots, shard, buf, sems)
            for c in copies:
                c.start()
            for c in copies:
                c.wait()


def layout_kernel(scal, block, near, far, give):
    step = pl.program_id(0)
    shard = far.shape[1]
    half = shard // 2
    give[0] = jnp.where(scal[0] == 0, block[0, half:], block[0, :half])
    for r in range(near.shape[1] // shard):

        @pl.when(step == r)
        def _():
            near[:, r * shard : (r + 1) * shard] = block[0].T

    @pl.when(step == pl.num_programs(0) - 1)
    def _():
        far[...] = block[0].T


def token_rows(scal, blocks):
    owners, shard, count = blocks.shape
    wide = (owners - 1) * shard
    return call(
        layout_kernel,
        "token_rows",
        0,
        6 * owners * shard * count,
        (scal, blocks),
        scalars=1,
        grid=(owners,),
        in_specs=[pl.BlockSpec((1, shard, count), lambda i, s: (s[1] ^ i, 0, 0))],
        out_specs=[
            pl.BlockSpec((count, wide), lambda i, s: (0, 0)),
            pl.BlockSpec((count, shard), lambda i, s: (0, 0)),
            pl.BlockSpec((1, shard // 2, count), lambda i, s: (i, 0, 0)),
        ],
        out_shape=[
            jax.ShapeDtypeStruct((count, wide), BF),
            jax.ShapeDtypeStruct((count, shard), BF),
            jax.ShapeDtypeStruct((owners, shard // 2, count), BF),
        ],
    )


def first_kernel(spots, shard, scal, tok, *refs):
    pieces = refs[: len(spots)]
    out, buf, sems = refs[len(spots) :]

    @pl.when(pl.program_id(0) == 0)
    def _():
        fetch(scal, pieces, spots, shard, buf, sems)

    out[...] = dot(tok[...], buf[...], 1, 0)


def key_kernel(spots, shard, scal, tok, part, *refs):
    pieces = refs[: len(spots)]
    k_out, kn_out, buf, sems = refs[len(spots) :]

    @pl.when(pl.program_id(0) == 0)
    def _():
        fetch(scal, pieces, spots, shard, buf, sems)
        kn_out[...] = jnp.zeros_like(kn_out)

    key = jnp.maximum(dot(tok[...], buf[...], 1, 0) + part[...], 0.0).astype(BF)
    k_out[:, : key.shape[1]] = key
    kn_out[...] += jnp.sum(key.astype(F32), axis=0, keepdims=True)


def val_kernel(spots, shard, scal, tok, part, k_ref, *refs):
    pieces = refs[: len(spots)]
    v_out, kv_out, buf, sems = refs[len(spots) :]

    @pl.when(pl.program_id(0) == 0)
    def _():
        fetch(scal, pieces, spots, shard, buf, sems)
        kv_out[...] = jnp.zeros_like(kv_out)

    width = buf.shape[1]
    v_out[:, :width] = (dot(tok[...], buf[...], 1, 0) + part[...]).astype(BF)
    for s, w in tiles_of(width):
        cols = slice(s, s + w)
        kv_out[:, cols] += fold(dot(v_out[:, cols], k_ref[:, cols], 0, 0), w)


def project(kernel, name, scal, tok, feats, pieces, spots, shard, state_rows, tile, wait=()):
    count, depth = tok.shape
    width = pieces[0].shape[1]
    rows = lambda w: pl.BlockSpec((tile, w), lambda i, s: (i, 0))
    kind, wide = (BF, padded(width)) if state_rows else (F32, width)
    return call(
        functools.partial(kernel, spots, shard),
        name,
        2 * count * depth * width,
        2 * (count * depth + depth * width + 3 * count * width),
        (scal, tok, *feats, *pieces),
        scalars=1,
        grid=(count // tile,),
        in_specs=[pl.BlockSpec((tile, depth), lambda i, s: (i, 0))]
        + [rows(x.shape[1]) for x in feats]
        + [pl.BlockSpec(memory_space=pltpu.HBM)] * len(pieces),
        out_specs=[rows(wide)] + [pl.BlockSpec((state_rows, width), lambda i, s: (0, 0))] * bool(state_rows),
        out_shape=[jax.ShapeDtypeStruct((count, wide), kind)]
        + [jax.ShapeDtypeStruct((state_rows, width), F32)] * bool(state_rows),
        scratch=[pltpu.VMEM((depth, width), BF), pltpu.SemaphoreType.DMA((len(pieces),))],
        wait=wait,
    )


def valid_rows(x, width):
    w = x.shape[0]
    return jnp.where(lax.broadcasted_iota(jnp.int32, (w, 1), 0) < width - pl.program_id(0) * w, x, 0)


def valid_lanes(x, width):
    w = x.shape[1]
    return jnp.where(lax.broadcasted_iota(jnp.int32, (1, w), 1) < width - pl.program_id(0) * w, x, 0)


def denominators(q, kn_row, w):
    high, low = split(jnp.where(same_head(w), jnp.broadcast_to(kn_row, (w, w)), 0.0))
    return 1.0 / (dot(high, q, 1, 0) + dot(low, q, 1, 0) + EPS_DEN)


def grad_kernel(width, q_ref, g_ref, kn, gs_out):
    w = q_ref.shape[0]
    q = valid_rows(jnp.maximum(q_ref[...], 0), width)
    g = valid_rows(g_ref[...], width).astype(F32)
    kn_row = valid_lanes(kn[...], width)
    dn = (g * denominators(q, kn_row, w)).astype(BF)
    gs_out[...] = fold(dot(dn, q, 1, 1), w)


def norm_kernel(width, q_ref, g_ref, kn, st, gn_out):
    w = q_ref.shape[0]
    q = valid_rows(jnp.maximum(q_ref[...], 0), width)
    g = valid_rows(g_ref[...], width).astype(F32)
    kn_row = valid_lanes(kn[...], width)
    kv_hi, kv_lo = split(unfold(valid_lanes(st[...], width), w))
    ones = jnp.where(same_head(w), 1.0, 0.0).astype(BF)
    inv = denominators(q, kn_row, w)
    attn = (dot(kv_hi, q, 1, 0) + dot(kv_lo, q, 1, 0)) * inv
    dden = -dot(ones, (g * attn).astype(BF), 1, 0) * inv
    gn = jnp.sum(dden * q.astype(F32), axis=1, keepdims=True)
    gn_out[...] = jnp.sum(jnp.where(diagonal(w), gn, 0.0), axis=0, keepdims=True)


def attend_kernel(width, q_ref, g_ref, kn, st, att_out, dq_out):
    w = q_ref.shape[0]
    q = valid_rows(jnp.maximum(q_ref[...], 0), width)
    g = valid_rows(g_ref[...], width).astype(F32)
    kn_row = valid_lanes(kn[...], width)
    kv = unfold(valid_lanes(st[...], width), w)
    kv_hi, kv_lo = split(kv)
    back_hi, back_lo = split(kv.T)
    kn_col = jnp.sum(jnp.where(diagonal(w), kn_row, 0.0), axis=1, keepdims=True)
    ones = jnp.where(same_head(w), 1.0, 0.0).astype(BF)

    inv = denominators(q, kn_row, w)
    attn = (dot(kv_hi, q, 1, 0) + dot(kv_lo, q, 1, 0)) * inv
    att_out[...] = attn.astype(BF)
    ga_hi, ga_lo = split(g * attn)
    dden = -(dot(ones, ga_hi, 1, 0) + dot(ones, ga_lo, 1, 0)) * inv
    dn_hi, dn_lo = split(g * inv)
    df = dot(back_hi, dn_hi, 1, 0) + dot(back_lo, dn_hi, 1, 0) + dot(back_hi, dn_lo, 1, 0)
    df = df + dden * kn_col
    dq_out[...] = jnp.where(q.astype(F32) > 0, df, 0.0).astype(BF)


def attention(kernel, name, queries, cotangent, states, n_big, state_rows, passes, wait=()):
    full, count = queries.shape
    row = pl.BlockSpec((LANES, count), lambda i: (i, 0))
    state = lambda r: pl.BlockSpec((r, LANES), lambda i: (0, i))
    return call(
        functools.partial(kernel, full),
        name,
        2 * passes * count * full * LANES,
        2 * (2 + n_big) * count * full,
        (queries, cotangent, *states),
        grid=(-(-full // LANES),),
        in_specs=[row, row] + [state(x.shape[0]) for x in states],
        out_specs=[row] * n_big + [state(state_rows)] * bool(state_rows),
        out_shape=[jax.ShapeDtypeStruct((full, count), BF)] * n_big
        + [jax.ShapeDtypeStruct((state_rows, full), F32)] * bool(state_rows),
        wait=wait,
    )


def dval_of(feats, states, scale, high, low, cols):
    (key,) = feats
    return dot(key[:, cols], high, 1, 1) + dot(key[:, cols], low, 1, 1)


def dkey_of(feats, states, scale, high, low, cols):
    key, val = feats
    d = dot(val[:, cols], high, 1, 0) + dot(val[:, cols], low, 1, 0) + states[1][:, cols] * scale
    return jnp.where(key[:, cols].astype(F32) > 0, d, 0.0)


def feature_grad(make, scale, feats, states, out):
    for s, w in tiles_of(states[0].shape[1]):
        cols = slice(s, s + w)
        high, low = split(unfold(states[0][:, cols] * scale, w))
        out[:, cols] = make(feats, states, scale, high, low, cols).astype(BF)


def feature_kernel(make, scale, n_feats, *refs):
    feature_grad(make, scale, refs[:n_feats], refs[n_feats:-1], refs[-1])


def feature_grads(make, name, feats, states, scale):
    count, wide = feats[0].shape
    return call(
        functools.partial(feature_kernel, make, scale, len(feats)),
        name,
        4 * count * wide * LANES,
        2 * count * wide * (1 + len(feats)),
        (*feats, *states),
        grid=(1,),
        in_specs=[pl.BlockSpec(x.shape, lambda i: (0, 0)) for x in (*feats, *states)],
        out_specs=[pl.BlockSpec((count, wide), lambda i: (0, 0))],
        out_shape=[jax.ShapeDtypeStruct((count, wide), BF)],
    )


def weight_kernel(make, scale, n_feats, n_states, scal, t_own, t_other, *refs):
    own, other = refs[:n_feats], refs[n_feats : 2 * n_feats]
    states = refs[2 * n_feats : 2 * n_feats + n_states]
    d_own, send_a, send_b, keep_a, keep_b, d_other = refs[2 * n_feats + n_states :]
    step = pl.program_id(0)

    @pl.when(step == 0)
    def _():
        feature_grad(make, scale, own, states, d_own)
        feature_grad(make, scale, other, states, d_other)

    cut, width = send_a.shape[1:]
    part = dot(t_own[0], d_own[:, :width], 1, 0) + dot(t_other[0], d_other[:, :width], 1, 0)
    a, b = part[:cut], part[cut:]

    @pl.when(step == 0)
    def _():
        send_a[1] = a.astype(BF)
        send_b[1] = b.astype(BF)

    @pl.when(step == 1)
    def _():
        send_b[0] = b.astype(BF)
        keep_a[1] = a

    @pl.when(step == 2)
    def _():
        send_a[0] = a.astype(BF)
        keep_b[1] = b

    @pl.when(step == 3)
    def _():
        keep_a[0] = a
        keep_b[0] = b


def weight_grads(make, name, scal, t_own, t_other, own, other, states, scale, wait=()):
    blocks, rows, count = t_other.shape
    wide, width = own[0].shape[1], states[0].shape[1]
    owned = pl.BlockSpec((1, rows, count), lambda i, s: (2 * (s[1] ^ (3 - i)) + s[0], 0, 0))
    others = pl.BlockSpec((1, rows, count), lambda i, s: (3 - i, 0, 0))
    whole = lambda x: pl.BlockSpec(x.shape, lambda i, s: (0, 0))
    full = lambda r: pl.BlockSpec((2, r, width), lambda i, s: (0, 0, 0))
    cut = (rows // 2 + 15) // 16 * 16
    rest = rows - cut
    return call(
        functools.partial(weight_kernel, make, scale, len(own), len(states)),
        name,
        4 * count * blocks * rows * width,
        4 * count * (blocks * rows + width * len(own)) + 3 * blocks * rows * width,
        (scal, t_own, t_other, *own, *other, *states),
        scalars=1,
        grid=(blocks,),
        in_specs=[owned, others] + [whole(x) for x in (*own, *other, *states)],
        out_specs=[whole(own[0]), full(cut), full(rest), full(cut), full(rest)],
        out_shape=[
            jax.ShapeDtypeStruct((count, wide), BF),
            jax.ShapeDtypeStruct((2, cut, width), BF),
            jax.ShapeDtypeStruct((2, rest, width), BF),
            jax.ShapeDtypeStruct((2, cut, width), F32),
            jax.ShapeDtypeStruct((2, rest, width), F32),
        ],
        scratch=[pltpu.VMEM((count, wide), BF)],
        wait=wait,
        vmem=48,
    )


def input_kernel(counts, spots, shard, scal, d_key, d_val, *refs):
    n = len(spots)
    keys, vals = refs[:n], refs[n : 2 * n]
    out, buf_k, buf_v, sems = refs[2 * n :]
    step = pl.program_id(0)

    def copies(core, k):
        at = sum(counts[:k])
        some = slice(at, at + counts[k])
        return [
            c
            for w, (pieces, buf) in enumerate(((keys, buf_k), (vals, buf_v)))
            for c in place(core, pieces[some], spots[some], shard, buf.at[k], sems.at[w, pl.ds(at, counts[k])])
        ]

    for core in (0, 1):

        @pl.when((scal[0] == core) & (step == 0))
        def _():
            for c in copies(core, 0):
                c.start()

        for k in range(len(counts)):

            @pl.when((scal[0] == core) & (step == k))
            def _():
                for c in copies(core, k + 1) if k + 1 < len(counts) else ():
                    c.start()
                for c in copies(core, k):
                    c.wait()

    width = buf_k.shape[2]
    total = dot(buf_k[step], d_key[:, :width], 1, 1) + dot(buf_v[step], d_val[:, :width], 1, 1)
    out[...] = total.astype(BF)


def input_grads(scal, d_key, d_val, keys, vals, spots, shard, depth, wait=()):
    count, width = d_key.shape[0], keys[0].shape[1]
    owners = depth // shard
    counts = tuple(sum(p[0] == k for p in spots) for k in range(owners))
    local = tuple((0,) + p[1:] for p in spots)
    whole = pl.BlockSpec(d_key.shape, lambda i, s: (0, 0))
    return call(
        functools.partial(input_kernel, counts, local, shard),
        "d_tokens",
        4 * count * depth * width,
        2 * depth * (count + 2 * width) + 4 * count * width,
        (scal, d_key, d_val, *keys, *vals),
        scalars=1,
        grid=(owners,),
        in_specs=[whole, whole] + [pl.BlockSpec(memory_space=pltpu.HBM)] * (len(keys) + len(vals)),
        out_specs=pl.BlockSpec((shard, count), lambda i, s: (s[1] ^ i, 0)),
        out_shape=jax.ShapeDtypeStruct((depth, count), BF),
        scratch=[
            pltpu.VMEM((owners, shard, width), BF),
            pltpu.VMEM((owners, shard, width), BF),
            pltpu.SemaphoreType.DMA((2, len(keys))),
        ],
        wait=wait,
        vmem=56,
    )


def swap(x, axis, bit):
    n = lax.axis_size(axis)
    return lax.ppermute(x, axis, [(i, i ^ bit) for i in range(n)])


def tile_of(count, sizes=(448, 128, 64, 32, 16)):
    return next(t for t in sizes if count % t == 0)


def together(*xs):
    return lax.optimization_barrier(xs)


def body_exchange(tokens, queries, w_key, w_value, cotangent):
    tok_t, qs, cot = tokens[0].T, queries[0].T, cotangent[0].T
    depth, count = tok_t.shape
    shard, full = w_key.shape
    tile = tile_of(count)
    img, spx = lax.axis_index("img"), lax.axis_index("sp")
    core, z = spx % 2, spx // 2
    scal = jnp.stack([core, img]).astype(jnp.int32)
    tok_img = count * lax.axis_size("sp")
    feat_scale = float(tok_img)
    scale = 1.0 / (lax.axis_size("img") * tok_img) ** 0.5

    span = span_of(shard)
    near = span // 32 * 16

    def near_rows(w):
        return jnp.where(core == 0, w[:span], w[shard - span :])

    def gather_near(own):
        return swap(own, "img", 1), swap(own, "img", 2)

    def gather_far(by_x, by_y):
        return swap(by_y[:near], "img", 1), swap(by_x[near:], "img", 2)

    def with_other(*pieces):
        return [p for piece in pieces for p in (piece, swap(piece, "sp", 1))]

    near_spots = ((0, None, 0), (1, 0, 0), (1, 1, 0), (2, 0, 0), (2, 1, 0))
    far_spots = ((0, 0, 0), (0, 1, 0), (0, 0, near), (0, 1, near))
    spots = near_spots + tuple((3,) + p[1:] for p in far_spots)

    def add(x, bit):
        return x + swap(x, "sp", bit)

    def add_beside(x, bit, *beside):
        got, *beside = together(swap(x.astype(BF), "sp", bit), *beside)
        return (x + got.astype(F32), *beside)

    kx, ky = gather_near(near_rows(w_key))
    t_own = tok_t.reshape(2 * lax.axis_size("img"), shard // 2, count)
    tok_near, tok_far, t_give = token_rows(scal, tok_t.reshape(lax.axis_size("img"), shard, count))
    kx, ky, tok_near, tok_far, t_give = together(kx, ky, tok_near, tok_far, t_give)
    kfa, kfb = gather_far(kx, ky)
    keys_near = [w_key] + with_other(kx, ky)
    t_other = swap(t_give, "sp", 1)
    (k_part,) = project(first_kernel, "key_near", scal, tok_near, [], keys_near, near_spots, shard, 0, tile)
    kfa, kfb, k_part, v_own, t_other = together(kfa, kfb, k_part, near_rows(w_value), t_other)
    keys_far = with_other(kfa, kfb)
    vx, vy = gather_near(v_own)
    key, kn = project(key_kernel, "key_feat", scal, tok_far, [k_part], keys_far, far_spots, shard, 1, tile)
    kn, key = together(add(kn, 1), key)
    key_other = swap(key, "sp", 1)
    kn, vx, vy = together(add(add(kn, 2), 4), vx, vy)
    (gs,) = attention(grad_kernel, "grad_state", qs, cot, [kn], 0, HD, 4)
    vx, vy, gs = together(vx, vy, gs)
    vfa, vfb = gather_far(vx, vy)
    gs = add(gs, 1)
    vals_near = [w_value] + with_other(vx, vy)
    (v_part,) = project(
        first_kernel, "val_near", scal, tok_near, [], vals_near, near_spots, shard, 0, tile, [gs]
    )
    gs, v_part, vfa, vfb, key_other = add_beside(gs, 2, v_part, vfa, vfb, key_other)
    vals_far = with_other(vfa, vfb)
    val, kv = project(val_kernel, "val_feat", scal, tok_far, [v_part, key], vals_far, far_spots, shard, HD, tile)
    gs, val, kv = add_beside(gs, 4, val, kv)
    kv, val = together(add(kv, 1), val)
    val_other = swap(val, "sp", 1)

    def reduce_near(parts):
        send_a, send_b, keep_a, keep_b = parts
        return swap(send_a, "img", 1), swap(send_b, "img", 2), keep_a, keep_b

    def add_near(got_a, got_b, keep_a, keep_b):
        a, b = keep_a + got_a.astype(F32), keep_b + got_b.astype(F32)
        return a[0], b[0], a[1].astype(BF), b[1].astype(BF)

    def reduce_far(a, b, send_a, send_b):
        return a, b, swap(send_a, "img", 2), swap(send_b, "img", 1)

    def merge(a, b, ra, rb):
        rows = [a + ra.astype(F32), b + rb.astype(F32)]
        spare = jnp.zeros((-(shard // 2) % 32, full), F32)
        return jnp.concatenate(rows + [spare], axis=0)

    def reduce_z(own):
        quarters = own.reshape(4, own.shape[0] // 4, full)
        pick = lambda k: lax.dynamic_index_in_dim(quarters, z ^ k, 0, False)
        sends = [pick(k).astype(BF) for k in (1, 2, 3)]
        return pick(0), sends, [swap(x, "sp", 2 * k) for k, x in zip((1, 2, 3), sends)]

    def spread_z(mine, gots):
        for got in gots:
            mine = mine + got.astype(F32)
        mine = (mine * scale).astype(BF)
        return [mine] + [swap(mine, "sp", 2 * k) for k in (1, 2, 3)]

    z0, z1 = z % 2, z // 2

    def part_of(x, at):
        return lax.dynamic_index_in_dim(x.reshape(2, x.shape[0] // 2, full), at, 0, False)

    def joined(mine, other, bit):
        low = bit == 0
        return jnp.concatenate([jnp.where(low, mine, other), jnp.where(low, other, mine)], axis=0)

    def ordered(quarters):
        stack = jnp.stack(quarters)
        return jnp.concatenate([lax.dynamic_index_in_dim(stack, z ^ k, 0, False) for k in range(4)], axis=0)

    def assemble(own):
        own = own[: shard // 2]
        other = swap(own, "sp", 1)
        out = jnp.concatenate(
            [jnp.where(core == 0, own, other), jnp.where(core == 0, other, own)], axis=0
        )
        return out.astype(F32)

    gots = [swap(kv.astype(BF), "sp", 2 * k) for k in (1, 2, 3)]
    d_val, *parts_v = weight_grads(
        dval_of, "d_w_value", scal, t_own, t_other, [key], [key_other], [gs], feat_scale, [kv]
    )
    *gots, val_other, d_val, p0, p1, p2, p3 = together(*gots, val_other, d_val, *parts_v)
    parts_v = [p0, p1, p2, p3]
    for got in gots:
        kv = kv + got.astype(F32)
    near_v = reduce_near(parts_v)
    (gn,) = attention(norm_kernel, "grad_norm", qs, cot, [kn, kv], 0, 1, 5)
    gn = add(add(add(gn, 1), 2), 4)
    n0, n1, n2, n3, gn = together(*near_v, gn)
    half_v = add_near(n0, n1, n2, n3)
    d_key, *parts_k = weight_grads(
        dkey_of, "d_w_key", scal, t_own, t_other, [key, val], [key_other, val_other], [gs, gn], feat_scale,
        half_v[2:],
    )
    near_k = reduce_near(parts_k)
    far_v = reduce_far(*half_v)
    own_v = merge(*far_v)
    attended, d_queries = attention(
        attend_kernel, "attend", qs, cot, [kn, kv], 2, 0, 11, [parts_k[0], parts_k[1]]
    )
    half_z = part_of(own_v, z0)
    got_v = swap(part_of(own_v, 1 - z0).astype(BF), "sp", 2)
    *near_k, attended, got_v = together(*near_k, attended, got_v)
    half_k = add_near(*near_k)
    far_k = reduce_far(*half_k)
    half_z = half_z + got_v.astype(F32)
    got_v = swap(part_of(half_z, 1 - z1).astype(BF), "sp", 4)
    *far_k, got_v = together(*far_k, got_v)
    mine_k, sends_k, gots_k = reduce_z(merge(*far_k))
    quart_v = ((part_of(half_z, z1) + got_v.astype(F32)) * scale).astype(BF)
    got_v = swap(quart_v, "sp", 4)
    d_tokens = input_grads(
        scal, d_key, d_val, keys_near + keys_far, vals_near + vals_far, spots, shard, depth, sends_k + [quart_v]
    )
    *gots_k, d_tokens, got_v = together(*gots_k, d_tokens, got_v)
    quart_k = spread_z(mine_k, gots_k)
    half_v = joined(quart_v, got_v, z1)
    whole_v = joined(half_v, swap(half_v, "sp", 2), z0)
    d_w_value = assemble(whole_v)
    d_w_key = assemble(ordered(quart_k))
    return attended.T[None], d_tokens.T[None], d_queries.T[None], d_w_key, d_w_value


def body_general(tokens, queries, w_key, w_value, cotangent):
    tok, qs, cot = tokens[0], queries[0].T, cotangent[0].T
    count = tok.shape[0]
    full = w_key.shape[1]
    tile = tile_of(count)
    tok_img = count * lax.axis_size("sp")
    feat_scale = float(tok_img)
    scale = 1.0 / (lax.axis_size("img") * tok_img) ** 0.5
    keys, vals = (lax.all_gather(w, "img", axis=0, tiled=True) for w in (w_key, w_value))
    key = jnp.maximum(dot(tok, keys, 1, 0), 0.0).astype(BF)
    val = dot(tok, vals, 1, 0).astype(BF)
    by_head = (count, full // HD, HD)
    kv = jnp.einsum("thj,thi->jhi", val.reshape(by_head), key.reshape(by_head), preferred_element_type=F32)
    kv = lax.psum(kv.reshape(HD, full), "sp")
    kn = lax.psum(jnp.sum(key.astype(F32), axis=0, keepdims=True), "sp")
    (gs,) = attention(grad_kernel, "grad_state", qs, cot, [kn], 0, HD, 4)
    gs = lax.psum(gs, "sp")
    (d_val,) = feature_grads(dval_of, "d_value", [key], [gs], feat_scale)
    (gn,) = attention(norm_kernel, "grad_norm", qs, cot, [kn, kv], 0, 1, 5)
    attended, d_queries = attention(attend_kernel, "attend", qs, cot, [kn, kv], 2, 0, 11)
    gn = lax.psum(gn, "sp")
    (d_key,) = feature_grads(dkey_of, "d_key", [key, val], [gs, gn], feat_scale)
    back = [dot(w, d[:, :full], 1, 1) for w, d in ((keys, d_key), (vals, d_val))]
    d_tokens = (back[0] + back[1]).astype(BF)
    out = []
    for d in (d_key, d_val):
        part = lax.psum_scatter(dot(tok, d[:, :full], 0, 0), "img", scatter_dimension=0, tiled=True)
        out.append(lax.psum(part, "sp") * scale)
    return attended.T[None], d_tokens.T[None], d_queries.T[None], *out


def solution(mesh):
    in_specs = (
        P("img", "sp", None),
        P("img", "sp", None),
        P("img", None),
        P("img", None),
        P("img", "sp", None),
    )
    out_specs = (
        P("img", "sp", None),
        P("img", "sp", None),
        P("img", "sp", None),
        P("img", None),
        P("img", None),
    )
    cubes = mesh.shape["img"] == 4 and mesh.shape["sp"] == 8
    body = body_exchange if cubes else body_general
    return jax.shard_map(body, mesh=mesh, in_specs=in_specs, out_specs=out_specs, check_vma=False)
```
